256 devices in a mesh: dp: 32 (over y, z), tensor: 8 (over x, core).
Axes of the slice: x: 4, y: 4, z: 8, core: 2. Of those that a mesh axis runs over, the one named last changes fastest.
Arguments:
- query_residual: bfloat16 [2048, 4096], P('dp', 'tensor'), as said below
- query_hidden: bfloat16 [2048, 6144], P('dp', 'tensor'), may hold values from -6 to 6
- doc_residual: bfloat16 [4096, 4096], P('dp', 'tensor'), as said below
- doc_hidden: bfloat16 [4096, 6144], P('dp', 'tensor'), may hold values from -6 to 6
- down_weight: bfloat16 [6144, 4096], P('tensor'), may hold values from -0.078125 to 0.078125
- norm_gain: float32 [4096], replicated, may hold values from 0.5 to 2
- pos_index: int32 [2048], replicated, may hold values from 0 to 4095, as said below
- neg_index: int32 [2048], replicated, may hold values from 0 to 4095
Outputs:
- query_grad: bfloat16 [2048, 6144], P('dp', 'tensor')
- doc_grad: bfloat16 [4096, 6144], P('dp', 'tensor')
- loss: float32 [], replicated
The draws below stay inside these ranges and needn't reach their ends.
Inputs may be any that keep to these rules, and one draw needn't show every extreme that they name: pos_index and neg_index together name every document exactly once. `query_residual`: entries of either sign. `doc_residual`: entries of either sign.
All inputs are finite; a program needn't handle non-finite values.
Results may differ from the reference program's by a relative error of at most 0.025.
Values may be sent and summed in bfloat16 or wider, within the bound.
A program may use at most 64 MiB of HBM per device.

```python
import math
import jax
import jax.numpy as jnp
from jax import lax

D = 4096
FF = 6144
NQ = 2048
ND = 4096


def shared_order(key):
    return jax.random.permutation(jax.random.fold_in(key, 1), ND).astype(jnp.int32)


def shared_parts(key):
    themes = max(4, NQ // 64)
    order = shared_order(key)
    theme_of = jax.random.randint(jax.random.fold_in(key, 2), (NQ,), 0, themes).astype(jnp.int32)
    theme_vectors = jax.random.normal(jax.random.fold_in(key, 3), (themes, D), jnp.float32)
    query_cores = jax.random.normal(jax.random.fold_in(key, 4), (NQ, D), jnp.float32)
    col_scale = jnp.exp(jax.random.uniform(jax.random.fold_in(key, 5), (1, D), jnp.float32, jnp.log(0.3), jnp.log(3.0)))
    return (order, theme_of, theme_vectors, query_cores, col_scale)


def row_scales(key, rows, high):
    return jnp.exp(jax.random.uniform(key, (rows, 1), jnp.float32, 0.0, jnp.log(high)))


def draw_pos_index(key, part):
    order = shared_order(key)
    return order[:NQ]


def draw_neg_index(key, part):
    order = shared_order(key)
    return order[NQ:]


def draw_query_residual(key, part):
    order, theme_of, theme_vectors, query_cores, col_scale = shared_parts(key)
    key = jax.random.fold_in(key, 11)
    noise_key, row_key = jax.random.split(key)
    themed = 0.548 * theme_vectors[theme_of] + 0.5 * query_cores
    noise = jax.random.normal(noise_key, (NQ, D), jnp.float32)
    mixture = themed + 0.671 * noise
    values = mixture * row_scales(row_key, NQ, 10.0) * col_scale
    return values.astype(jnp.bfloat16)


def draw_doc_residual(key, part):
    order, theme_of, theme_vectors, query_cores, col_scale = shared_parts(key)
    key = jax.random.fold_in(key, 13)
    noise_key, row_key = jax.random.split(key)
    slot_of = jnp.zeros((ND,), jnp.int32).at[order].set(jnp.arange(ND, dtype=jnp.int32))
    owner = slot_of % NQ
    positive = (slot_of < NQ).astype(jnp.float32)[:, None]
    core_weight = 0.5 * positive + 0.25 * (1.0 - positive)
    themed = 0.548 * theme_vectors[theme_of[owner]] + core_weight * query_cores[owner]
    noise = jax.random.normal(noise_key, (ND, D), jnp.float32)
    noise_weight = 0.671 * positive + 0.798 * (1.0 - positive)
    mixture = themed + noise_weight * noise
    values = mixture * row_scales(row_key, ND, 10.0) * col_scale
    return values.astype(jnp.bfloat16)


def levels(rng, extent, cuts, smallest, largest):
    loudness = 1.0
    for axis_at, parts in cuts:
        heights = jax.random.uniform(jax.random.fold_in(jax.random.fold_in(rng, 6), axis_at), (parts,), jnp.float32, smallest / len(cuts), largest / len(cuts))
        loudness = loudness * jnp.repeat(jnp.exp(heights), extent[axis_at] // parts).reshape((-1,) + (1,) * (len(extent) - 1 - axis_at))
    return loudness


def scatter_about(key, extent, spread, most, pieces=(), kind=jnp.bfloat16):
    values = jax.random.normal(key, extent, jnp.float32) * spread
    if len(pieces) > 0:
        values = levels(key, extent, pieces, -0.22, 0.18) * values
    return jnp.clip(values, min=-most, max=most).astype(kind)


def setup_inputs(seed: int = 0) -> dict:
    keys = jax.random.split(jax.random.key(seed), 9)
    return {
        "query_residual": draw_query_residual(jax.random.fold_in(keys[8], 71), 0),
        "query_hidden": scatter_about(keys[1], (NQ, FF), 1.0, 6.0, ((0, 32), (1, 8))),
        "doc_residual": draw_doc_residual(jax.random.fold_in(keys[8], 71), 0),
        "doc_hidden": scatter_about(keys[3], (ND, FF), 1.0, 6.0, ((0, 32), (1, 8))),
        "down_weight": scatter_about(keys[4], (FF, D), FF ** -0.5, 0.078125, ((0, 8),)),
        "norm_gain": jnp.clip(jnp.exp(jax.random.uniform(keys[5], (D,), jnp.float32, math.log(0.5), math.log(2.0))), 0.5, 2.0),
        "pos_index": draw_pos_index(jax.random.fold_in(keys[8], 71), 0),
        "neg_index": draw_neg_index(jax.random.fold_in(keys[8], 71), 0),
    }


EPS = 1e-06
TAU = 0.05
LOSS_SCALE = 256.0

def embed(residual, hidden, down_weight, norm_gain):
    outputs = residual.astype(jnp.float32) + jnp.dot(hidden, down_weight, preferred_element_type=jnp.float32)
    scaled = outputs * norm_gain
    inverse = lax.rsqrt(lax.optimization_barrier(jnp.sum(scaled * scaled, 1, keepdims=True)) + EPS)
    return (scaled * inverse, inverse)

def backward(unit, inverse, grads, norm_gain, down_weight):
    alignment = lax.optimization_barrier(jnp.sum(unit * grads, 1, keepdims=True))
    grad_pre = (norm_gain * ((grads - unit * alignment) * inverse)).astype(jnp.bfloat16)
    return jnp.dot(grad_pre, down_weight.T, preferred_element_type=jnp.float32).astype(jnp.bfloat16)

def reference(query_residual, query_hidden, doc_residual, doc_hidden, down_weight, norm_gain, pos_index, neg_index):
    q_unit, q_inverse = embed(query_residual, query_hidden, down_weight, norm_gain)
    d_unit, d_inverse = embed(doc_residual, doc_hidden, down_weight, norm_gain)
    q_emb = q_unit.astype(jnp.bfloat16)
    d_emb = d_unit.astype(jnp.bfloat16)
    scores = jnp.dot(q_emb, d_emb.T, preferred_element_type=jnp.float32) * (1.0 / TAU)
    expo = jnp.exp(scores)
    total = lax.optimization_barrier(jnp.sum(expo, 1))
    prob = expo / total[:, None]
    column = jnp.arange(ND, dtype=jnp.int32)
    pos_hot = (column[None, :] == pos_index[:, None]).astype(jnp.float32)
    neg_hot = (column[None, :] == neg_index[:, None]).astype(jnp.float32)
    s_pos = lax.optimization_barrier(jnp.sum(scores * pos_hot, 1))
    s_neg = lax.optimization_barrier(jnp.sum(scores * neg_hot, 1))
    margin = s_neg - s_pos
    sig = jax.nn.sigmoid(margin)
    loss = jnp.mean(jnp.log(total) - s_pos + jax.nn.softplus(margin))
    coef = (LOSS_SCALE / TAU * (prob - pos_hot * (1.0 + sig)[:, None] + neg_hot * sig[:, None])).astype(jnp.bfloat16)
    grad_q = jnp.dot(coef, d_emb, preferred_element_type=jnp.float32)
    grad_d = jnp.dot(coef.T, q_emb, preferred_element_type=jnp.float32)
    query_grad = backward(q_unit, q_inverse, grad_q, norm_gain, down_weight)
    doc_grad = backward(d_unit, d_inverse, grad_d, norm_gain, down_weight)
    return (query_grad, doc_grad, loss)
```

```python
import functools

import jax
import jax.numpy as jnp
from jax import lax
from jax.experimental import pallas as pl
from jax.experimental.pallas import tpu as pltpu
from jax.sharding import PartitionSpec as P

EPS = 1e-06
TAU = 0.05
LOSS_SCALE = 256.0
NX, NY, NZ = 4, 4, 8
NT = 2 * NX
MESH = pl.DeviceIdType.MESH
F32 = jnp.float32
BF16 = jnp.bfloat16


def dot_nn(a, b):
    return lax.dot_general(a, b, (((1,), (0,)), ((), ())), preferred_element_type=F32)


def dot_nt(a, b):
    return lax.dot_general(a, b, (((1,), (1,)), ((), ())), preferred_element_type=F32)


def eye(n, m, shift=0):
    rows = lax.broadcasted_iota(jnp.int32, (n, m), 0)
    cols = lax.broadcasted_iota(jnp.int32, (n, m), 1)
    return cols == rows + shift


def to_row(col):
    n = col.shape[0]
    return jnp.sum(jnp.where(eye(n, n), col, 0.0), axis=0, keepdims=True)


def to_col(row):
    n = row.shape[1]
    return jnp.sum(jnp.where(eye(n, n), row, 0.0), axis=1, keepdims=True)


def rows8(*rows):
    width = rows[0].shape[1]
    index = lax.broadcasted_iota(jnp.int32, (8, width), 0)
    out = jnp.zeros((8, width), F32)
    for i, row in enumerate(rows):
        out = jnp.where(index == i, row, out)
    return out


def pad_lanes(row, width):
    return jnp.concatenate([row, jnp.zeros((1, width - row.shape[1]), F32)], axis=1)


class Ids:
    def __init__(self):
        self.n = 0

    def take(self, n):
        base = self.n
        self.n += n
        return base


RID = Ids()
R_SIB, R_XQ, R_XD = RID.take(4), RID.take(4), RID.take(4)
R_ZQ, R_YD = RID.take(8), RID.take(4)
R_SSIB, R_SX = RID.take(4), RID.take(4)
R_STAT = RID.take(8)
R_CF = RID.take(8)
R_GQ, R_GD = RID.take(8), RID.take(4)
R_KD, R_KQ = RID.take(8), RID.take(8)
R_PD, R_PQ = RID.take(8), RID.take(8)
R_LOSS = RID.take(4)
N_SEND = 112
X_ORDER = (2, 1, 3)
Z_ORDER = (4, 3, 5, 2, 6, 1, 7)
Y_ORDER = (2, 1, 3)


def kernel(
    nq, nd, q_res, q_hid, d_res, d_hid, w_hbm, gain_ref, pos_ref, neg_ref,
    q_out, d_out, loss_out,
    hid, res, wv, s1, r1, s2, r2, acc, scf, qall, dall, sS, rS, s3, r3, stats,
    cf, ct, sq, rq, sd, rd, kd, kq, gp, ly, back, local, send, recv,
):
    dp = lax.axis_index("dp")
    t = lax.axis_index("tensor")
    x, c = t // 2, t % 2
    y, z = dp // NZ, dp % NZ

    def at_x(k):
        return (dp, 2 * ((x + k) % NX) + c)

    def at_t(k):
        return (dp, (t + k) % NT)

    def at_y(k):
        return (((y + k) % NY) * NZ + z, t)

    def at_z(k):
        return (y * NZ + (z + k) % NZ, t)

    sib = (dp, 2 * x + 1 - c)
    sends = []

    def push(src, dst, rid, device):
        copy = pltpu.make_async_remote_copy(
            src_ref=src, dst_ref=dst, send_sem=send.at[len(sends)], recv_sem=recv.at[rid],
            device_id=device, device_id_type=MESH,
        )
        copy.start()
        sends.append(copy)

    def got(dst, rid, device):
        pltpu.make_async_remote_copy(
            src_ref=dst, dst_ref=dst, send_sem=send.at[0], recv_sem=recv.at[rid],
            device_id=device, device_id_type=MESH,
        ).wait_recv()

    loads = []

    def load(src, dst):
        copy = pltpu.make_async_copy(src, dst, local.at[len(loads)])
        copy.start()
        loads.append(copy)
        return copy

    h_loads = [load(q_hid, hid.at[pl.ds(0, nq)]), load(d_hid, hid.at[pl.ds(nq, nd)])]
    x_all = X_ORDER + (0,)
    w_loads = {}
    width = res.shape[1]
    for a in (1, 0):
        for k in x_all:
            owner = 2 * ((x + k) % NX) + (c + a) % 2
            columns = pl.ds(pl.multiple_of(owner * width, width), width)
            w_loads[a, k] = load(w_hbm.at[:, columns], wv.at[4 * a + k])
    r_loads = [load(q_res, res.at[pl.ds(0, nq)]), load(d_res, res.at[pl.ds(nq, nd)])]

    barrier = pltpu.get_barrier_semaphore()
    peers = [at_t(k) for k in range(1, NT)] + [at_z(k) for k in range(1, NZ)]
    peers += [at_y(k) for k in range(1, NY)]
    for peer in peers:
        pl.semaphore_signal(barrier, inc=1, device_id=peer, device_id_type=MESH)

    for copy in h_loads:
        copy.wait()
    for i, k in enumerate(x_all):
        w_loads[1, k].wait()
        s1[k] = dot_nn(hid[...], wv[4 + k]).astype(BF16)
        if i == 0:
            pl.semaphore_wait(barrier, len(peers))
        push(s1.at[k], r1.at[k], R_SIB + k, sib)
    q_rows, d_rows = pl.ds(0, nq), pl.ds(nq, nd)
    for k in X_ORDER:
        w_loads[0, k].wait()
        part = dot_nn(hid[...], wv[k])
        got(r1.at[k], R_SIB + k, sib)
        s2[k - 1] = (part + r1[k].astype(F32)).astype(BF16)
        push(s2.at[k - 1, q_rows], r2.at[3 - k, q_rows], R_XQ + 4 - k, at_x(k))
    for k in X_ORDER:
        push(s2.at[k - 1, d_rows], r2.at[3 - k, d_rows], R_XD + 4 - k, at_x(k))
    w_loads[0, 0].wait()
    part = dot_nn(hid[...], wv[0])
    got(r1.at[0], R_SIB, sib)
    acc[...] = part + r1[0].astype(F32)
    for copy in r_loads:
        copy.wait()
    gain = gain_ref[t]

    for k in X_ORDER:
        got(r2.at[k - 1, q_rows], R_XQ + k, at_x(k))
    total = acc[0:nq] + res[0:nq].astype(F32)
    for k in (1, 2, 3):
        total = total + r2[k - 1, 0:nq].astype(F32)
    scaled = total * gain
    scf[0:nq] = scaled
    qall[z] = scaled.astype(BF16)
    for k in Z_ORDER:
        push(qall.at[z], qall.at[z], R_ZQ + 8 - k, at_z(k))
    for k in X_ORDER:
        got(r2.at[k - 1, d_rows], R_XD + k, at_x(k))
    total = acc[nq:] + res[nq:].astype(F32)
    for k in (1, 2, 3):
        total = total + r2[k - 1, nq:].astype(F32)
    scaled = total * gain
    scf[nq:] = scaled
    dall[y] = scaled.astype(BF16)
    for k in Y_ORDER:
        push(dall.at[y], dall.at[y], R_YD + 4 - k, at_y(k))
    own_ss_q = to_row(jnp.sum(scf[0:nq] * scf[0:nq], axis=1, keepdims=True))
    own_ss_d = to_row(jnp.sum(scf[nq:] * scf[nq:], axis=1, keepdims=True))

    for k in Y_ORDER:
        got(dall.at[(y + k) % NY], R_YD + k, at_y(k))
    all_d = NY * nd
    pieces = []
    for k in range(NY):
        rows = dall[k].astype(F32)
        pieces.append(to_row(jnp.sum(rows * rows, axis=1, keepdims=True)))
    ss_d = jnp.concatenate(pieces, axis=1)
    for k in Z_ORDER:
        got(qall.at[(z + k) % NZ], R_ZQ + k, at_z(k))

    def block(owner):
        rows = qall[owner]
        scores = dot_nt(rows, dall[...].reshape(all_d, width))
        wide = rows.astype(F32)
        ss_q = to_row(jnp.sum(wide * wide, axis=1, keepdims=True))
        return scores, rows8(pad_lanes(ss_q, all_d), ss_d)

    for k in x_all:
        scores, tail = block(2 * ((x + k) % NX) + 1 - c)
        sS[k, 0:nq] = scores
        sS[k, nq:] = tail
        push(sS.at[k], rS.at[k], R_SSIB + k, sib)
    for k in X_ORDER:
        scores, tail = block(2 * ((x + k) % NX) + c)
        got(rS.at[k], R_SSIB + k, sib)
        s3[k, 0:nq] = scores + rS[k, 0:nq]
        s3[k, nq:] = tail + rS[k, nq:]
        push(s3.at[k], r3.at[3 - k], R_SX + 4 - k, at_x(k))
    scores, tail = block(t)
    got(rS.at[0], R_SSIB, sib)
    s3[0, 0:nq] = scores + rS[0, 0:nq]
    s3[0, nq:] = tail + rS[0, nq:]
    for k in X_ORDER:
        got(r3.at[k - 1], R_SX + k, at_x(k))
    full = s3[0] + r3[0] + r3[1] + r3[2]

    inv_d = lax.rsqrt(full[nq + 1 : nq + 2] + EPS)
    inv_q = lax.rsqrt(to_col(full[nq : nq + 1, 0:nq]) + EPS)
    scores = full[0:nq] * inv_q * inv_d * (1.0 / TAU)
    expo = jnp.exp(scores)
    lanes = lax.broadcasted_iota(jnp.int32, (1, all_d), 1)
    column = ((lanes // nd) * NZ + z) * nd + lanes % nd
    group = (y * NZ + t) * nq
    row_at, shift = group // 128, group % 128
    pick = eye(nq, 128, shift)
    pos = jnp.sum(jnp.where(pick, pos_ref[row_at].astype(F32), 0.0), axis=1, keepdims=True)
    neg = jnp.sum(jnp.where(pick, neg_ref[row_at].astype(F32), 0.0), axis=1, keepdims=True)
    pos_hot = column == pos.astype(jnp.int32)
    neg_hot = column == neg.astype(jnp.int32)
    stats[z] = rows8(
        pad_lanes(to_row(jnp.sum(expo, axis=1, keepdims=True)), 128),
        pad_lanes(to_row(jnp.sum(jnp.where(pos_hot, scores, 0.0), axis=1, keepdims=True)), 128),
        pad_lanes(to_row(jnp.sum(jnp.where(neg_hot, scores, 0.0), axis=1, keepdims=True)), 128),
    )
    for k in Z_ORDER:
        push(stats.at[z], stats.at[z], R_STAT + 8 - k, at_z(k))
    for k in Z_ORDER:
        got(stats.at[(z + k) % NZ], R_STAT + k, at_z(k))
    stat = stats[0]
    for k in range(1, NZ):
        stat = stat + stats[k]
    tot_row, pos_row, neg_row = stat[0:1, 0:nq], stat[1:2, 0:nq], stat[2:3, 0:nq]
    margin = neg_row - pos_row
    soft = jnp.maximum(margin, 0.0) + jnp.log1p(jnp.exp(-jnp.abs(margin)))
    loss_part = jnp.sum(jnp.log(tot_row) - pos_row + soft, axis=1, keepdims=True)
    low = jnp.exp(-jnp.abs(margin))
    sig_row = jnp.where(margin >= 0.0, 1.0, low) / (1.0 + low)
    sig = to_col(sig_row)
    coef = expo / to_col(tot_row)
    coef = jnp.where(pos_hot, coef - (1.0 + sig), coef)
    coef = jnp.where(neg_hot, coef + sig, coef)
    cf[t] = ((LOSS_SCALE / TAU) * coef * inv_q * inv_d).astype(BF16)

    def gather_start(ref, rid):
        for k in X_ORDER:
            push(ref(t), ref(t), rid + 4 - k, at_x(k))
        push(ref(t), ref(t), rid, sib)

    def gather_pass(ref, rid):
        for k in X_ORDER:
            slot = ref(2 * ((x + k) % NX) + c)
            got(slot, rid + k, at_x(k))
            push(slot, slot, rid + 4 + k, sib)

    def gather_got(ref, rid, k):
        got(ref(2 * ((x + k) % NX) + 1 - c), rid + (4 + k if k else 0), sib)

    gather_start(lambda i: cf.at[i], R_CF)
    gather_pass(lambda i: cf.at[i], R_CF)
    for k in x_all:
        gather_got(lambda i: cf.at[i], R_CF, k)

    for k in Z_ORDER:
        sq[k - 1] = dot_nn(cf[(z + k) % NZ], dall[...].reshape(all_d, width)).astype(BF16)
        push(sq.at[k - 1], rq.at[7 - k], R_GQ + 8 - k, at_z(k))
    all_q = NZ * nq
    ct[...] = cf[...].reshape(all_q, all_d).T.reshape(NY, nd, all_q)
    for k in Y_ORDER:
        sd[k - 1] = dot_nn(ct[(y + k) % NY], qall[...].reshape(all_q, width)).astype(BF16)
        push(sd.at[k - 1], rd.at[3 - k], R_GD + 4 - k, at_y(k))
    grad_d = dot_nn(ct[y], qall[...].reshape(all_q, width))
    acc[0:nq] = dot_nn(cf[z], dall[...].reshape(all_d, width))

    def project_out(buffer, rid, raw, rows, own_ss, extra):
        kappa = to_row(jnp.sum(scf[rows] * raw, axis=1, keepdims=True))
        n = kappa.shape[1]
        tall = [kappa, own_ss] + extra
        buffer[t] = rows8(*[pad_lanes(r, 128) if r.shape[1] < 128 else r for r in tall])
        for k in range(1, NT):
            push(buffer.at[t], buffer.at[t], rid + 8 - k, at_t(k))
        for k in range(1, NT):
            got(buffer.at[(t + k) % NT], rid + k, at_t(k))
        summed = buffer[0]
        for k in range(1, NT):
            summed = summed + buffer[k]
        factor = to_col(summed[0:1, 0:n] / (summed[1:2, 0:n] + EPS))
        return (gain * (raw - scf[rows] * factor)).astype(BF16), summed

    for k in Y_ORDER:
        got(rd.at[k - 1], R_GD + k, at_y(k))
    for k in (1, 2, 3):
        grad_d = grad_d + rd[k - 1].astype(F32)
    loss_row = jnp.broadcast_to(loss_part, (1, 128))
    pre, summed = project_out(kd, R_KD, grad_d, slice(nq, nq + nd), own_ss_d, [loss_row])
    gp[t, nq:] = pre
    gather_start(lambda i: gp.at[i, d_rows], R_PD)
    ly[y] = summed
    for k in Y_ORDER:
        push(ly.at[y], ly.at[y], R_LOSS + 4 - k, at_y(k))

    for k in Z_ORDER:
        got(rq.at[k - 1], R_GQ + k, at_z(k))
    grad_q = acc[0:nq]
    for k in range(1, NZ):
        grad_q = grad_q + rq[k - 1].astype(F32)
    pre, _ = project_out(kq, R_KQ, grad_q, slice(0, nq), own_ss_q, [])
    gp[t, 0:nq] = pre
    gather_start(lambda i: gp.at[i, q_rows], R_PQ)

    gather_pass(lambda i: gp.at[i, d_rows], R_PD)
    gather_pass(lambda i: gp.at[i, q_rows], R_PQ)
    order = [(0, 0), (1, 0)] + [(a, k) for k in X_ORDER for a in (0, 1)]
    for rid, rows, out in ((R_PD, d_rows, d_out), (R_PQ, q_rows, q_out)):
        result = None
        for a, k in order:
            if a:
                gather_got(lambda i: gp.at[i, rows], rid, k)
            owner = 2 * ((x + k) % NX) + (c + a) % 2
            term = dot_nt(gp[owner, rows], wv[4 * a + k])
            result = term if result is None else result + term
        out[...] = result.astype(BF16)

    for k in Y_ORDER:
        got(ly.at[(y + k) % NY], R_LOSS + k, at_y(k))
    whole = ly[0] + ly[1] + ly[2] + ly[3]
    loss_out[0, 0] = jnp.sum(whole[2:3, 0:1]) * (1.0 / (NY * NZ * nq))
    for copy in sends:
        copy.wait_send()


def shards(
    query_residual, query_hidden, doc_residual, doc_hidden, down_weight, norm_gain, pos_index, neg_index,
):
    nq, width = query_residual.shape
    nd = doc_residual.shape[0]
    depth = query_hidden.shape[1]
    n = nq + nd
    all_q, all_d = NZ * nq, NY * nd
    anywhere = pl.BlockSpec(memory_space=pl.ANY)
    vmem = pl.BlockSpec(memory_space=pltpu.VMEM)
    query_grad, doc_grad, loss = pl.pallas_call(
        functools.partial(kernel, nq, nd),
        out_shape=(
            jax.ShapeDtypeStruct((nq, depth), BF16),
            jax.ShapeDtypeStruct((nd, depth), BF16),
            jax.ShapeDtypeStruct((1, 1), F32),
        ),
        in_specs=[anywhere] * 5 + [vmem] * 3,
        out_specs=(vmem, vmem, pl.BlockSpec(memory_space=pltpu.SMEM)),
        scratch_shapes=[
            pltpu.VMEM((n, depth), BF16),
            pltpu.VMEM((n, width), BF16),
            pltpu.VMEM((NT, depth, width), BF16),
            pltpu.VMEM((NX, n, width), BF16),
            pltpu.VMEM((NX, n, width), BF16),
            pltpu.VMEM((NX - 1, n, width), BF16),
            pltpu.VMEM((NX - 1, n, width), BF16),
            pltpu.VMEM((n, width), F32),
            pltpu.VMEM((n, width), F32),
            pltpu.VMEM((NZ, nq, width), BF16),
            pltpu.VMEM((NY, nd, width), BF16),
            pltpu.VMEM((NX, nq + 8, all_d), F32),
            pltpu.VMEM((NX, nq + 8, all_d), F32),
            pltpu.VMEM((NX, nq + 8, all_d), F32),
            pltpu.VMEM((NX - 1, nq + 8, all_d), F32),
            pltpu.VMEM((NZ, 8, 128), F32),
            pltpu.VMEM((NT, nq, all_d), BF16),
            pltpu.VMEM((NY, nd, all_q), BF16),
            pltpu.VMEM((NZ - 1, nq, width), BF16),
            pltpu.VMEM((NZ - 1, nq, width), BF16),
            pltpu.VMEM((NY - 1, nd, width), BF16),
            pltpu.VMEM((NY - 1, nd, width), BF16),
            pltpu.VMEM((NT, 8, 128), F32),
            pltpu.VMEM((NT, 8, 128), F32),
            pltpu.VMEM((NT, n, width), BF16),
            pltpu.VMEM((NY, 8, 128), F32),
            pltpu.VMEM((n, depth), F32),
            pltpu.SemaphoreType.DMA((12,)),
            pltpu.SemaphoreType.DMA((N_SEND,)),
            pltpu.SemaphoreType.DMA((RID.n,)),
        ],
        compiler_params=pltpu.CompilerParams(
            collective_id=0, has_side_effects=True, vmem_limit_bytes=48 * 2**20
        ),
        name="step",
    )(
        query_residual, query_hidden, doc_residual, doc_hidden, down_weight,
        norm_gain.reshape(NT, 1, width), pos_index.reshape(-1, 1, 128), neg_index.reshape(-1, 1, 128),
    )
    return query_grad, doc_grad, loss.reshape(())


def solution(mesh):
    placed = (
        P("dp", "tensor"),
        P("dp", "tensor"),
        P("dp", "tensor"),
        P("dp", "tensor"),
        P("tensor", None),
        P(),
        P(),
        P(),
    )
    return jax.shard_map(
        shards,
        mesh=mesh,
        in_specs=placed,
        out_specs=(P("dp", "tensor"), P("dp", "tensor"), P()),
        check_vma=False,
    )
```

```python
import functools

import jax
import jax.numpy as jnp
from jax import lax
from jax.experimental import pallas as pl
from jax.experimental.pallas import tpu as pltpu
from jax.sharding import PartitionSpec as P

EPS = 1e-06
TAU = 0.05
LOSS_SCALE = 256.0
NX, NY, NZ = 4, 4, 8
NT = 2 * NX
MESH = pl.DeviceIdType.MESH
F32 = jnp.float32
BF16 = jnp.bfloat16


def dot_nn(a, b):
    return lax.dot_general(a, b, (((1,), (0,)), ((), ())), preferred_element_type=F32)


def dot_nt(a, b):
    return lax.dot_general(a, b, (((1,), (1,)), ((), ())), preferred_element_type=F32)


def eye(n, m, shift=0):
    rows = lax.broadcasted_iota(jnp.int32, (n, m), 0)
    cols = lax.broadcasted_iota(jnp.int32, (n, m), 1)
    return cols == rows + shift


def to_row(col):
    n = col.shape[0]
    return jnp.sum(jnp.where(eye(n, n), col, 0.0), axis=0, keepdims=True)


def to_col(row):
    n = row.shape[1]
    return jnp.sum(jnp.where(eye(n, n), row, 0.0), axis=1, keepdims=True)


def rows8(*rows):
    width = rows[0].shape[1]
    index = lax.broadcasted_iota(jnp.int32, (8, width), 0)
    out = jnp.zeros((8, width), F32)
    for i, row in enumerate(rows):
        out = jnp.where(index == i, row, out)
    return out


def pad_lanes(row, width):
    return jnp.concatenate([row, jnp.zeros((1, width - row.shape[1]), F32)], axis=1)


class Ids:
    def __init__(self):
        self.n = 0

    def take(self, n):
        base = self.n
        self.n += n
        return base


RID = Ids()
R_SIB, R_XQ, R_XD = RID.take(4), RID.take(4), RID.take(4)
R_ZQ, R_ZH, R_YD = RID.take(8), RID.take(1), RID.take(4)
R_SSIB, R_SX = RID.take(4), RID.take(4)
R_STAT = RID.take(8)
R_CF = RID.take(8)
R_G1, R_GH, R_GQ, R_GD = RID.take(2), RID.take(2), RID.take(8), RID.take(4)
R_KZ, R_KT, R_KD, R_KY = RID.take(8), RID.take(8), RID.take(8), RID.take(4)
R_PD, R_PQ = RID.take(8), RID.take(8)
N_SEND = 112
X_ORDER = (2, 1, 3)
Z_ORDER = (4, 3, 5, 2, 6, 1, 7)
Y_ORDER = (2, 1, 3)


def kernel(
    nq, nd, q_res, q_hid, d_res, d_hid, w_hbm, gain_hbm, pos_hbm, neg_hbm,
    out, loss_out,
    gain_ref, pos_ref, neg_ref, hid, res, wv, wt, s1, r1, s2, r2, acc, qall, dall, sS, rS, s3, r3, stats,
    cf, ct, sq, hold, rq1, rqh, rq, sd, rd, kz, kt, kd, kds, ky, gp, local, send, recv,
):
    dp = lax.axis_index("dp")
    t = lax.axis_index("tensor")
    x, c = t // 2, t % 2
    y, z = dp // NZ, dp % NZ

    def at_x(k):
        return (dp, 2 * ((x + k) % NX) + c)

    def at_t(k):
        return (dp, (t + k) % NT)

    def at_y(k):
        return (((y + k) % NY) * NZ + z, t)

    def at_z(k):
        return (y * NZ + (z + k) % NZ, t)

    sib = (dp, 2 * x + 1 - c)
    sends = []

    def push(src, dst, rid, device):
        copy = pltpu.make_async_remote_copy(
            src_ref=src, dst_ref=dst, send_sem=send.at[len(sends)], recv_sem=recv.at[rid],
            device_id=device, device_id_type=MESH,
        )
        copy.start()
        sends.append(copy)

    def got(dst, rid, device):
        pltpu.make_async_remote_copy(
            src_ref=dst, dst_ref=dst, send_sem=send.at[0], recv_sem=recv.at[rid],
            device_id=device, device_id_type=MESH,
        ).wait_recv()

    def turn(first, last):
        for i in range(first, last):
            wt[i] = wv[i].T

    loads = []

    def load(src, dst):
        copy = pltpu.make_async_copy(src, dst, local.at[len(loads)])
        copy.start()
        loads.append(copy)
        return copy

    h_loads = [load(q_hid, hid.at[pl.ds(0, nq)]), load(d_hid, hid.at[pl.ds(nq, nd)])]
    x_all = X_ORDER + (0,)
    w_loads = {}
    width = res.shape[1]
    for a in (1, 0):
        for k in x_all:
            owner = 2 * ((x + k) % NX) + (c + a) % 2
            columns = pl.ds(pl.multiple_of(owner * width, width), width)
            w_loads[a, k] = load(w_hbm.at[:, columns], wv.at[4 * a + k])
    r_loads = [load(gain_hbm, gain_ref), load(pos_hbm, pos_ref), load(neg_hbm, neg_ref)]
    r_loads += [load(q_res, res.at[pl.ds(0, nq)]), load(d_res, res.at[pl.ds(nq, nd)])]

    barrier = pltpu.get_barrier_semaphore()
    peers = [at_t(k) for k in range(1, NT)] + [at_z(k) for k in range(1, NZ)]
    peers += [at_y(k) for k in range(1, NY)]
    for peer in peers:
        pl.semaphore_signal(barrier, inc=1, device_id=peer, device_id_type=MESH)

    for copy in h_loads:
        copy.wait()
    for i, k in enumerate(x_all):
        w_loads[1, k].wait()
        s1[k] = dot_nn(hid[...], wv[4 + k]).astype(BF16)
        if i == 0:
            pl.semaphore_wait(barrier, len(peers))
        push(s1.at[k], r1.at[k], R_SIB + k, sib)
    q_rows, d_rows = pl.ds(0, nq), pl.ds(nq, nd)
    for k in X_ORDER:
        w_loads[0, k].wait()
        part = dot_nn(hid[...], wv[k])
        got(r1.at[k], R_SIB + k, sib)
        s2[k - 1] = (part + r1[k].astype(F32)).astype(BF16)
        push(s2.at[k - 1, q_rows], r2.at[3 - k, q_rows], R_XQ + 4 - k, at_x(k))
    for k in X_ORDER:
        push(s2.at[k - 1, d_rows], r2.at[3 - k, d_rows], R_XD + 4 - k, at_x(k))
    w_loads[0, 0].wait()
    part = dot_nn(hid[...], wv[0])
    got(r1.at[0], R_SIB, sib)
    acc[...] = part + r1[0].astype(F32)
    for copy in r_loads:
        copy.wait()
    gain = gain_ref[t]

    for k in X_ORDER:
        got(r2.at[k - 1, q_rows], R_XQ + k, at_x(k))
    total = acc[0:nq] + res[0:nq].astype(F32)
    for k in (1, 2, 3):
        total = total + r2[k - 1, 0:nq].astype(F32)
    qall[z] = (total * gain).astype(BF16)
    for k in (2, 6, 1, 7):
        push(qall.at[z], qall.at[z], R_ZQ + 8 - k, at_z(k))
    turn(0, 2)
    for k in X_ORDER:
        got(r2.at[k - 1, d_rows], R_XD + k, at_x(k))
    total = acc[nq:] + res[nq:].astype(F32)
    for k in (1, 2, 3):
        total = total + r2[k - 1, nq:].astype(F32)
    dall[y] = (total * gain).astype(BF16)
    for k in Y_ORDER:
        push(dall.at[y], dall.at[y], R_YD + 4 - k, at_y(k))
    half = nq // 2
    halves = {2: pl.ds(0, half), 6: pl.ds(half, half)}
    for k in (2, 6):
        slot = (z + k) % NZ
        got(qall.at[slot], R_ZQ + k, at_z(k))
        push(qall.at[slot], qall.at[slot], R_ZQ + (3 if k == 2 else 5), at_z(7 if k == 2 else 1))
        part = qall.at[slot, halves[k]]
        push(part, part, R_ZQ + 4 if k == 2 else R_ZH, at_z(8 - k))
    turn(2, 4)

    for k in Y_ORDER:
        got(dall.at[(y + k) % NY], R_YD + k, at_y(k))
    all_d = NY * nd
    pieces = []
    for k in range(NY):
        rows = dall[k].astype(F32)
        pieces.append(to_row(jnp.sum(rows * rows, axis=1, keepdims=True)))
    ss_d = jnp.concatenate(pieces, axis=1)
    for k in (1, 7, 3, 5):
        got(qall.at[(z + k) % NZ], R_ZQ + k, at_z(k))
    slot = (z + 4) % NZ
    got(qall.at[slot, halves[2]], R_ZQ + 4, at_z(2))
    got(qall.at[slot, halves[6]], R_ZH, at_z(6))

    def block(owner):
        rows = qall[owner]
        scores = dot_nt(rows, dall[...].reshape(all_d, width))
        wide = rows.astype(F32)
        ss_q = to_row(jnp.sum(wide * wide, axis=1, keepdims=True))
        return scores, rows8(pad_lanes(ss_q, all_d), ss_d)

    for k in x_all:
        scores, tail = block(2 * ((x + k) % NX) + 1 - c)
        sS[k, 0:nq] = scores
        sS[k, nq:] = tail
        push(sS.at[k], rS.at[k], R_SSIB + k, sib)
    for k in X_ORDER:
        scores, tail = block(2 * ((x + k) % NX) + c)
        got(rS.at[k], R_SSIB + k, sib)
        s3[k, 0:nq] = scores + rS[k, 0:nq]
        s3[k, nq:] = tail + rS[k, nq:]
        push(s3.at[k], r3.at[3 - k], R_SX + 4 - k, at_x(k))
    scores, tail = block(t)
    got(rS.at[0], R_SSIB, sib)
    s3[0, 0:nq] = scores + rS[0, 0:nq]
    s3[0, nq:] = tail + rS[0, nq:]
    turn(4, 6)
    for k in X_ORDER:
        got(r3.at[k - 1], R_SX + k, at_x(k))
    full = s3[0] + r3[0] + r3[1] + r3[2]

    inv_d = lax.rsqrt(full[nq + 1 : nq + 2] + EPS)
    inv_q_row = lax.rsqrt(full[nq : nq + 1, 0:nq] + EPS)
    inv_q = to_col(inv_q_row)
    scores = full[0:nq] * inv_q * inv_d * (1.0 / TAU)
    expo = jnp.exp(scores)
    lanes = lax.broadcasted_iota(jnp.int32, (1, all_d), 1)
    column = ((lanes // nd) * NZ + z) * nd + lanes % nd
    group = (y * NZ + t) * nq
    row_at, shift = group // 128, group % 128
    pick = eye(nq, 128, shift)
    pos = jnp.sum(jnp.where(pick, pos_ref[row_at].astype(F32), 0.0), axis=1, keepdims=True)
    neg = jnp.sum(jnp.where(pick, neg_ref[row_at].astype(F32), 0.0), axis=1, keepdims=True)
    pos_hot = column == pos.astype(jnp.int32)
    neg_hot = column == neg.astype(jnp.int32)
    stats[z] = rows8(
        pad_lanes(to_row(jnp.sum(expo, axis=1, keepdims=True)), 128),
        pad_lanes(to_row(jnp.sum(jnp.where(pos_hot, scores, 0.0), axis=1, keepdims=True)), 128),
        pad_lanes(to_row(jnp.sum(jnp.where(neg_hot, scores, 0.0), axis=1, keepdims=True)), 128),
    )
    for k in Z_ORDER:
        push(stats.at[z], stats.at[z], R_STAT + 8 - k, at_z(k))
    turn(6, 8)
    for k in Z_ORDER:
        got(stats.at[(z + k) % NZ], R_STAT + k, at_z(k))
    stat = stats[0]
    for k in range(1, NZ):
        stat = stat + stats[k]
    tot_row, pos_row, neg_row = stat[0:1, 0:nq], stat[1:2, 0:nq], stat[2:3, 0:nq]
    margin = neg_row - pos_row
    soft = jnp.maximum(margin, 0.0) + jnp.log1p(jnp.exp(-jnp.abs(margin)))
    loss_part = jnp.sum(jnp.log(tot_row) - pos_row + soft, axis=1, keepdims=True)
    low = jnp.exp(-jnp.abs(margin))
    sig_row = jnp.where(margin >= 0.0, 1.0, low) / (1.0 + low)
    sig = to_col(sig_row)
    coef = expo / to_col(tot_row)
    coef = jnp.where(pos_hot, coef - (1.0 + sig), coef)
    coef = jnp.where(neg_hot, coef + sig, coef)
    coef = ((LOSS_SCALE / TAU) * coef * inv_q * inv_d).astype(BF16)
    cf[t] = coef

    def gather_start(ref, rid):
        for k in X_ORDER:
            push(ref(t), ref(t), rid + 4 - k, at_x(k))
        push(ref(t), ref(t), rid, sib)

    def gather_pass(ref, rid):
        for k in X_ORDER:
            slot = ref(2 * ((x + k) % NX) + c)
            got(slot, rid + k, at_x(k))
            push(slot, slot, rid + 4 + k, sib)

    def gather_got(ref, rid, k):
        got(ref(2 * ((x + k) % NX) + 1 - c), rid + (4 + k if k else 0), sib)

    gather_start(lambda i: cf.at[i], R_CF)

    inner = coef.astype(F32) * full[0:nq]
    kz[z] = rows8(pad_lanes(to_row(jnp.sum(inner, axis=1, keepdims=True)), 128))
    kd[t] = rows8(jnp.sum(inner, axis=0, keepdims=True), jnp.broadcast_to(loss_part, (1, all_d)))
    for k in Z_ORDER:
        push(kz.at[z], kz.at[z], R_KZ + 8 - k, at_z(k))
    for k in range(1, NT):
        push(kd.at[t], kd.at[t], R_KD + 8 - k, at_t(k))
    gather_pass(lambda i: cf.at[i], R_CF)
    for k in x_all:
        gather_got(lambda i: cf.at[i], R_CF, k)

    def grad_q(k):
        return dot_nn(cf[(z + k) % NZ], dall[...].reshape(all_d, width))

    for i, k in enumerate((3, 5)):
        sq[i] = grad_q(k).astype(BF16)
        push(sq.at[i], rq1.at[i], R_G1 + i, at_z(1 if k == 3 else 7))
    sq[2] = grad_q(4).astype(BF16)
    push(sq.at[2, halves[2]], rqh.at[0], R_GH, at_z(2))
    push(sq.at[2, halves[6]], rqh.at[1], R_GH + 1, at_z(6))
    for i, k in enumerate((1, 7)):
        sq[3 + i] = grad_q(k).astype(BF16)
        push(sq.at[3 + i], rq.at[1 - i], R_GQ + 8 - k, at_z(k))
    for i, k in enumerate((2, 6)):
        hold[i] = grad_q(k)
    all_q = NZ * nq
    ct[...] = cf[...].reshape(all_q, all_d).T.reshape(NY, nd, all_q)
    for k in Y_ORDER:
        sd[k - 1] = dot_nn(ct[(y + k) % NY], qall[...].reshape(all_q, width)).astype(BF16)
        push(sd.at[k - 1], rd.at[3 - k], R_GD + 4 - k, at_y(k))
    for i, k in enumerate((2, 6)):
        got(rq1.at[i], R_G1 + i, at_z(7 if k == 2 else 1))
        got(rqh.at[i], R_GH + i, at_z(8 - k))
        low = slice(0, half) if k == 2 else slice(half, nq)
        high = slice(half, nq) if k == 2 else slice(0, half)
        summed = hold[i] + rq1[i].astype(F32)
        sq[5 + i, low] = (summed[low] + rqh[i].astype(F32)).astype(BF16)
        sq[5 + i, high] = summed[high].astype(BF16)
        push(sq.at[5 + i], rq.at[3 - i], R_GQ + 8 - k, at_z(k))
    grad_d = dot_nn(ct[y], qall[...].reshape(all_q, width))
    acc[0:nq] = grad_q(0)

    for k in range(1, NT):
        got(kd.at[(t + k) % NT], R_KD + k, at_t(k))
    summed = kd[0]
    for k in range(1, NT):
        summed = summed + kd[k]
    summed = rows8(summed[0:1], summed[1:2], inv_d * inv_d)
    for k in range(NY):
        kds[k] = summed[:, k * nd : (k + 1) * nd]
    for k in Y_ORDER:
        push(kds.at[(y + k) % NY], ky.at[y], R_KY + 4 - k, at_y(k))
    ky[y] = kds[y]
    for k in Z_ORDER:
        got(kz.at[(z + k) % NZ], R_KZ + k, at_z(k))
    summed = kz[0]
    for k in range(1, NZ):
        summed = summed + kz[k]
    kt[t] = rows8(pad_lanes(summed[0:1, 0:nq] * inv_q_row * inv_q_row, 128))
    for k in range(1, NT):
        push(kt.at[t], kt.at[t], R_KT + 8 - k, at_t(k))

    for k in Y_ORDER:
        got(rd.at[k - 1], R_GD + k, at_y(k))
    for k in (1, 2, 3):
        grad_d = grad_d + rd[k - 1].astype(F32)
    for k in Y_ORDER:
        got(ky.at[(y + k) % NY], R_KY + k, at_y(k))
    summed = ky[0] + ky[1] + ky[2] + ky[3]
    loss_out[0, 0] = jnp.sum(summed[1:2, 0:1]) * (1.0 / (NY * NZ * nq))
    inverse2 = kds[y]
    factor = to_col(summed[0:1] * inverse2[2:3])
    gp[t, nq:] = (gain * (grad_d - dall[y].astype(F32) * factor)).astype(BF16)
    gather_start(lambda i: gp.at[i, d_rows], R_PD)

    for i, k in enumerate((1, 7, 2, 6)):
        got(rq.at[i], R_GQ + k, at_z(k))
    for k in range(1, NT):
        got(kt.at[(t + k) % NT], R_KT + k, at_t(k))
    grad = acc[0:nq]
    for i in range(4):
        grad = grad + rq[i].astype(F32)
    factor = kt[z]
    factor = to_col(factor[0:1, 0:nq])
    gp[t, 0:nq] = (gain * (grad - qall[z].astype(F32) * factor)).astype(BF16)
    gather_start(lambda i: gp.at[i, q_rows], R_PQ)

    gather_pass(lambda i: gp.at[i, d_rows], R_PD)
    result = None
    for a in (0, 1):
        for k in (0,) + X_ORDER:
            if a:
                gather_got(lambda i: gp.at[i, d_rows], R_PD, k)
            owner = 2 * ((x + k) % NX) + (c + a) % 2
            term = dot_nn(gp[owner, nq:], wt[4 * a + k])
            result = term if result is None else result + term
    out[nq:] = result.astype(BF16)
    result = None
    for a in (0, 1):
        for k in (0,) + X_ORDER:
            owner = 2 * ((x + k) % NX) + (c + a) % 2
            if a:
                gather_got(lambda i: gp.at[i, q_rows], R_PQ, k)
            elif k:
                slot = gp.at[owner, q_rows]
                got(slot, R_PQ + k, at_x(k))
                push(slot, slot, R_PQ + 4 + k, sib)
            term = dot_nn(gp[owner, 0:nq], wt[4 * a + k])
            result = term if result is None else result + term
    out[0:nq] = result.astype(BF16)
    for copy in sends:
        copy.wait_send()


def shards(
    query_residual, query_hidden, doc_residual, doc_hidden, down_weight, norm_gain, pos_index, neg_index,
):
    nq, width = query_residual.shape
    nd = doc_residual.shape[0]
    depth = query_hidden.shape[1]
    n = nq + nd
    all_q, all_d = NZ * nq, NY * nd
    hbm = pl.BlockSpec(memory_space=pltpu.HBM)
    vmem = pl.BlockSpec(memory_space=pltpu.VMEM)
    grads, loss = pl.pallas_call(
        functools.partial(kernel, nq, nd),
        out_shape=(jax.ShapeDtypeStruct((n, depth), BF16), jax.ShapeDtypeStruct((1, 1), F32)),
        in_specs=[hbm] * 8,
        out_specs=(vmem, pl.BlockSpec(memory_space=pltpu.SMEM)),
        scratch_shapes=[
            pltpu.VMEM((NT, 1, width), F32),
            pltpu.VMEM((NZ * NY * nq // 128, 1, 128), jnp.int32),
            pltpu.VMEM((NZ * NY * nq // 128, 1, 128), jnp.int32),
            pltpu.VMEM((n, depth), BF16),
            pltpu.VMEM((n, width), BF16),
            pltpu.VMEM((NT, depth, width), BF16),
            pltpu.VMEM((NT, width, depth), BF16),
            pltpu.VMEM((NX, n, width), BF16),
            pltpu.VMEM((NX, n, width), BF16),
            pltpu.VMEM((NX - 1, n, width), BF16),
            pltpu.VMEM((NX - 1, n, width), BF16),
            pltpu.VMEM((n, width), F32),
            pltpu.VMEM((NZ, nq, width), BF16),
            pltpu.VMEM((NY, nd, width), BF16),
            pltpu.VMEM((NX, nq + 8, all_d), F32),
            pltpu.VMEM((NX, nq + 8, all_d), F32),
            pltpu.VMEM((NX, nq + 8, all_d), F32),
            pltpu.VMEM((NX - 1, nq + 8, all_d), F32),
            pltpu.VMEM((NZ, 8, 128), F32),
            pltpu.VMEM((NT, nq, all_d), BF16),
            pltpu.VMEM((NY, nd, all_q), BF16),
            pltpu.VMEM((NZ - 1, nq, width), BF16),
            pltpu.VMEM((2, nq, width), F32),
            pltpu.VMEM((2, nq, width), BF16),
            pltpu.VMEM((2, nq // 2, width), BF16),
            pltpu.VMEM((4, nq, width), BF16),
            pltpu.VMEM((NY - 1, nd, width), BF16),
            pltpu.VMEM((NY - 1, nd, width), BF16),
            pltpu.VMEM((NZ, 8, 128), F32),
            pltpu.VMEM((NT, 8, 128), F32),
            pltpu.VMEM((NT, 8, all_d), F32),
            pltpu.VMEM((NY, 8, nd), F32),
            pltpu.VMEM((NY, 8, nd), F32),
            pltpu.VMEM((NT, n, width), BF16),
            pltpu.SemaphoreType.DMA((16,)),
            pltpu.SemaphoreType.DMA((N_SEND,)),
            pltpu.SemaphoreType.DMA((RID.n,)),
        ],
        compiler_params=pltpu.CompilerParams(
            collective_id=0, has_side_effects=True, vmem_limit_bytes=63 * 2**20
        ),
        name="step",
    )(
        query_residual, query_hidden, doc_residual, doc_hidden, down_weight,
        norm_gain.reshape(NT, 1, width), pos_index.reshape(-1, 1, 128), neg_index.reshape(-1, 1, 128),
    )
    return grads[:nq], grads[nq:], loss.reshape(())


def solution(mesh):
    placed = (
        P("dp", "tensor"),
        P("dp", "tensor"),
        P("dp", "tensor"),
        P("dp", "tensor"),
        P("tensor", None),
        P(),
        P(),
        P(),
    )
    return jax.shard_map(
        shards,
        mesh=mesh,
        in_specs=placed,
        out_specs=(P("dp", "tensor"), P("dp", "tensor"), P()),
        check_vma=False,
    )
```

```python
import functools

import jax
import jax.numpy as jnp
from jax import lax
from jax.experimental import pallas as pl
from jax.experimental.pallas import tpu as pltpu
from jax.sharding import PartitionSpec as P

EPS = 1e-06
TAU = 0.05
LOSS_SCALE = 256.0
NX, NY, NZ = 4, 4, 8
NT = 2 * NX
MESH = pl.DeviceIdType.MESH
F32 = jnp.float32
BF16 = jnp.bfloat16


def dot_nn(a, b):
    return lax.dot_general(a, b, (((1,), (0,)), ((), ())), preferred_element_type=F32)


def dot_nt(a, b):
    return lax.dot_general(a, b, (((1,), (1,)), ((), ())), preferred_element_type=F32)


def eye(n, m, shift=0):
    rows = lax.broadcasted_iota(jnp.int32, (n, m), 0)
    cols = lax.broadcasted_iota(jnp.int32, (n, m), 1)
    return cols == rows + shift


def to_row(col):
    n = col.shape[0]
    return jnp.sum(jnp.where(eye(n, n), col, 0.0), axis=0, keepdims=True)


def to_col(row):
    n = row.shape[1]
    return jnp.sum(jnp.where(eye(n, n), row, 0.0), axis=1, keepdims=True)


def rows8(*rows):
    width = rows[0].shape[1]
    index = lax.broadcasted_iota(jnp.int32, (8, width), 0)
    out = jnp.zeros((8, width), F32)
    for i, row in enumerate(rows):
        out = jnp.where(index == i, row, out)
    return out


def pad_lanes(row, width):
    return jnp.concatenate([row, jnp.zeros((1, width - row.shape[1]), F32)], axis=1)


class Ids:
    def __init__(self):
        self.n = 0

    def take(self, n):
        base = self.n
        self.n += n
        return base


RID = Ids()
R_SQ, R_SD = RID.take(4), RID.take(4)
R_XQ, R_XD = RID.take(4), (RID.take(4), RID.take(4))
R_ZQ, R_ZH, R_QS = RID.take(8), RID.take(1), RID.take(8)
R_YD, R_DS = (RID.take(4), RID.take(4)), (RID.take(4), RID.take(4))
R_SX = RID.take(4)
R_STAT, R_ROW = RID.take(8), RID.take(8)
R_CF = RID.take(8)
R_G1, R_GH, R_GQ, R_GD = RID.take(2), RID.take(2), RID.take(8), RID.take(4)
R_KZ, R_KT, R_KD, R_KY = RID.take(8), RID.take(8), RID.take(8), RID.take(4)
R_PD, R_PQ = RID.take(8), RID.take(8)
N_SEND = 160
X_ORDER = (2, 1, 3)
Z_ORDER = (4, 3, 5, 2, 6, 1, 7)
Y_ORDER = (2, 1, 3)


def kernel(
    nq, nd, q_res, q_hid, d_res, d_hid, w_hbm, gain_hbm, pos_hbm, neg_hbm,
    out, loss_out,
    gain_ref, pos_ref, neg_ref, hid, res, wv, wt, s1, r1, s2, r2, acc, qall, qs, dall, ds, s3, r3, stats,
    row, hot, cf, cg, ct, sq, hold, rq1, rqh, rq, sd, rd, kz, kt, kd, kds, ky, gp, local, send, recv,
):
    dp = lax.axis_index("dp")
    t = lax.axis_index("tensor")
    x, c = t // 2, t % 2
    y, z = dp // NZ, dp % NZ

    def at_x(k):
        return (dp, 2 * ((x + k) % NX) + c)

    def at_t(k):
        return (dp, (t + k) % NT)

    def at_y(k):
        return (((y + k) % NY) * NZ + z, t)

    def at_z(k):
        return (y * NZ + (z + k) % NZ, t)

    sib = (dp, 2 * x + 1 - c)
    sends = []

    def push(src, dst, rid, device):
        copy = pltpu.make_async_remote_copy(
            src_ref=src, dst_ref=dst, send_sem=send.at[len(sends)], recv_sem=recv.at[rid],
            device_id=device, device_id_type=MESH,
        )
        copy.start()
        sends.append(copy)

    def got(dst, rid, device):
        pltpu.make_async_remote_copy(
            src_ref=dst, dst_ref=dst, send_sem=send.at[0], recv_sem=recv.at[rid],
            device_id=device, device_id_type=MESH,
        ).wait_recv()

    def turn(first, last):
        for i in range(first, last):
            wt[i] = wv[i].T

    loads = []

    def load(src, dst):
        copy = pltpu.make_async_copy(src, dst, local.at[len(loads)])
        copy.start()
        loads.append(copy)
        return copy

    h_loads = [load(q_hid, hid.at[pl.ds(0, nq)]), load(d_hid, hid.at[pl.ds(nq, nd)])]
    x_all = X_ORDER + (0,)
    w_loads = {}
    width = res.shape[1]
    for a in (1, 0):
        for k in x_all:
            owner = 2 * ((x + k) % NX) + (c + a) % 2
            columns = pl.ds(pl.multiple_of(owner * width, width), width)
            w_loads[a, k] = load(w_hbm.at[:, columns], wv.at[4 * a + k])
    r_loads = [load(gain_hbm, gain_ref), load(pos_hbm, pos_ref), load(neg_hbm, neg_ref)]
    r_loads += [load(q_res, res.at[pl.ds(0, nq)]), load(d_res, res.at[pl.ds(nq, nd)])]

    barrier = pltpu.get_barrier_semaphore()
    peers = [at_t(k) for k in range(1, NT)] + [at_z(k) for k in range(1, NZ)]
    peers += [at_y(k) for k in range(1, NY)]
    for peer in peers:
        pl.semaphore_signal(barrier, inc=1, device_id=peer, device_id_type=MESH)

    for copy in h_loads:
        copy.wait()
    q_rows, d_rows = pl.ds(0, nq), pl.ds(nq, nd)
    d_parts = [pl.ds(nq + i * (nd // 2), nd // 2) for i in range(2)]
    for i, k in enumerate(x_all):
        w_loads[1, k].wait()
        s1[k, 0:nq] = dot_nn(hid[0:nq], wv[4 + k]).astype(BF16)
        if i == 0:
            pl.semaphore_wait(barrier, len(peers))
        push(s1.at[k, q_rows], r1.at[k, q_rows], R_SQ + k, sib)
    for k in x_all:
        w_loads[0, k].wait()
        part = dot_nn(hid[0:nq], wv[k])
        got(r1.at[k, q_rows], R_SQ + k, sib)
        part = part + r1[k, 0:nq].astype(F32)
        if k:
            s2[k - 1, 0:nq] = part.astype(BF16)
            push(s2.at[k - 1, q_rows], r2.at[3 - k, q_rows], R_XQ + 4 - k, at_x(k))
        else:
            acc[0:nq] = part
    for k in x_all:
        s1[k, nq:] = dot_nn(hid[nq:], wv[4 + k]).astype(BF16)
        push(s1.at[k, d_rows], r1.at[k, d_rows], R_SD + k, sib)
    for k in x_all:
        part = dot_nn(hid[nq:], wv[k])
        got(r1.at[k, d_rows], R_SD + k, sib)
        part = part + r1[k, nq:].astype(F32)
        if k:
            s2[k - 1, nq:] = part.astype(BF16)
            push(s2.at[k - 1, d_parts[0]], r2.at[3 - k, d_parts[0]], R_XD[0] + 4 - k, at_x(k))
        else:
            acc[nq:] = part
    for k in X_ORDER:
        push(s2.at[k - 1, d_parts[1]], r2.at[3 - k, d_parts[1]], R_XD[1] + 4 - k, at_x(k))
    for copy in r_loads:
        copy.wait()
    gain = gain_ref[t]

    parity = (z + c + 1) % 2
    passed = []

    def pass_q(k):
        slot = (z + k) % NZ
        copy = pltpu.make_async_remote_copy(
            src_ref=qall.at[slot], dst_ref=qs.at[slot], send_sem=send.at[N_SEND - 8 + k],
            recv_sem=recv.at[R_QS + k], device_id=sib, device_id_type=MESH,
        )
        passed.append((k, copy))

        @pl.when(parity == k % 2)
        def _():
            copy.start()

    def full_rows(rows):
        total = acc[rows] + res[rows].astype(F32)
        for k in (1, 2, 3):
            total = total + r2[k - 1, rows].astype(F32)
        return (total * gain).astype(BF16)

    for k in X_ORDER:
        got(r2.at[k - 1, q_rows], R_XQ + k, at_x(k))
    qall[z] = full_rows(slice(0, nq))
    for k in (2, 6, 1, 7):
        push(qall.at[z], qall.at[z], R_ZQ + 8 - k, at_z(k))
    pass_q(0)
    turn(0, 2)
    for i in range(2):
        for k in X_ORDER:
            got(r2.at[k - 1, d_parts[i]], R_XD[i] + k, at_x(k))
        low = i * (nd // 2)
        dall[y, low : low + nd // 2] = full_rows(slice(nq + low, nq + low + nd // 2))
        slot = dall.at[y, pl.ds(low, nd // 2)]
        for k in Y_ORDER:
            push(slot, slot, R_YD[i] + 4 - k, at_y(k))
        push(slot, ds.at[y, pl.ds(low, nd // 2)], R_DS[i], sib)
    half = nq // 2
    halves = {2: pl.ds(0, half), 6: pl.ds(half, half)}
    for k in (2, 6):
        slot = (z + k) % NZ
        got(qall.at[slot], R_ZQ + k, at_z(k))
        push(qall.at[slot], qall.at[slot], R_ZQ + (3 if k == 2 else 5), at_z(7 if k == 2 else 1))
        part = qall.at[slot, halves[k]]
        push(part, part, R_ZQ + 4 if k == 2 else R_ZH, at_z(8 - k))
        pass_q(k)
    for k in (1, 7):
        got(qall.at[(z + k) % NZ], R_ZQ + k, at_z(k))
        pass_q(k)
    all_d = NY * nd
    lanes = lax.broadcasted_iota(jnp.int32, (1, all_d), 1)
    column = ((lanes // nd) * NZ + z) * nd + lanes % nd
    for i in range(NZ):
        at = y * (NZ * nq // 128) + i * nq // 128
        pick = eye(nq, 128, i * nq % 128)
        pos = jnp.sum(jnp.where(pick, pos_ref[at].astype(F32), 0.0), axis=1, keepdims=True)
        neg = jnp.sum(jnp.where(pick, neg_ref[at].astype(F32), 0.0), axis=1, keepdims=True)
        mark = jnp.where(column == neg.astype(jnp.int32), 2.0, 0.0)
        hot[i] = jnp.where(column == pos.astype(jnp.int32), 1.0, mark)
    turn(2, 4)

    for i in range(2):
        for k in Y_ORDER:
            slot = (y + k) % NY
            place = pl.ds(i * (nd // 2), nd // 2)
            got(dall.at[slot, place], R_YD[i] + k, at_y(k))
            push(dall.at[slot, place], ds.at[slot, place], R_DS[i] + k, sib)
    for k in (3, 5):
        got(qall.at[(z + k) % NZ], R_ZQ + k, at_z(k))
        pass_q(k)
    slot = (z + 4) % NZ
    got(qall.at[slot, halves[2]], R_ZQ + 4, at_z(2))
    got(qall.at[slot, halves[6]], R_ZH, at_z(6))
    pass_q(4)

    for i in range(2):
        for k in (0,) + Y_ORDER:
            got(ds.at[(y + k) % NY, pl.ds(i * (nd // 2), nd // 2)], R_DS[i] + k, sib)

    def squares(*blocks):
        total = 0.0
        for rows in blocks:
            wide = rows.astype(F32)
            total = total + wide * wide
        return to_row(jnp.sum(total, axis=1, keepdims=True))

    ss_d = jnp.concatenate([squares(dall[k], ds[k]) for k in range(NY)], axis=1)
    for k in range(NZ):

        @pl.when(parity != k % 2)
        def _(k=k):
            got(qs.at[(z + k) % NZ], R_QS + k, sib)

    for k in x_all:
        owner = 2 * ((x + k) % NX) + c
        rows, other = qall[owner], qs[owner]
        scores = dot_nt(rows, dall[...].reshape(all_d, width))
        scores = scores + dot_nt(other, ds[...].reshape(all_d, width))
        s3[k, 0:nq] = scores
        s3[k, nq:] = rows8(pad_lanes(squares(rows, other), all_d), ss_d)
        if k:
            push(s3.at[k], r3.at[3 - k], R_SX + 4 - k, at_x(k))
    turn(4, 6)
    for k in X_ORDER:
        got(r3.at[k - 1], R_SX + k, at_x(k))
    full = s3[0] + r3[0] + r3[1] + r3[2]

    inv_d = lax.rsqrt(full[nq + 1 : nq + 2] + EPS)
    inv_q_row = lax.rsqrt(full[nq : nq + 1, 0:nq] + EPS)
    inv_q = to_col(inv_q_row)
    scores = full[0:nq] * inv_q * inv_d * (1.0 / TAU)
    expo = jnp.exp(scores)
    marks = hot[t]
    pos_hot, neg_hot = marks == 1.0, marks == 2.0
    stats[z] = rows8(
        pad_lanes(to_row(jnp.sum(expo, axis=1, keepdims=True)), 128),
        pad_lanes(to_row(jnp.sum(jnp.where(pos_hot, scores, 0.0), axis=1, keepdims=True)), 128),
        pad_lanes(to_row(jnp.sum(jnp.where(neg_hot, scores, 0.0), axis=1, keepdims=True)), 128),
    )
    def gather_start(ref, rid):
        for k in X_ORDER:
            push(ref(t), ref(t), rid + 4 - k, at_x(k))
        push(ref(t), ref(t), rid, sib)

    def gather_pass(ref, rid):
        for k in X_ORDER:
            slot = ref(2 * ((x + k) % NX) + c)
            got(slot, rid + k, at_x(k))
            push(slot, slot, rid + 4 + k, sib)

    def gather_got(ref, rid, k):
        got(ref(2 * ((x + k) % NX) + 1 - c), rid + (4 + k if k else 0), sib)

    for k in Z_ORDER:
        push(stats.at[z], stats.at[z], R_STAT + 8 - k, at_z(k))
    cf[t] = (expo * inv_d).astype(BF16)
    gather_start(lambda i: cf.at[i], R_CF)
    turn(6, 8)
    for k in Z_ORDER:
        got(stats.at[(z + k) % NZ], R_STAT + k, at_z(k))
    stat = stats[0]
    for k in range(1, NZ):
        stat = stat + stats[k]
    tot_row, pos_row, neg_row = stat[0:1, 0:nq], stat[1:2, 0:nq], stat[2:3, 0:nq]
    margin = neg_row - pos_row
    low = jnp.exp(-jnp.abs(margin))
    sig = jnp.where(margin >= 0.0, 1.0, low) / (1.0 + low)
    scale = (LOSS_SCALE / TAU) * inv_q_row
    row[t] = rows8(
        pad_lanes(scale / tot_row, 128),
        pad_lanes(scale * (jnp.exp(pos_row) / tot_row - (1.0 + sig)), 128),
        pad_lanes(scale * (jnp.exp(neg_row) / tot_row + sig), 128),
    )
    for k in range(1, NT):
        push(row.at[t], row.at[t], R_ROW + 8 - k, at_t(k))
    soft = jnp.maximum(margin, 0.0) + jnp.log1p(low)
    loss_part = jnp.sum(jnp.log(tot_row) - pos_row + soft, axis=1, keepdims=True)
    gather_pass(lambda i: cf.at[i], R_CF)
    for k in range(1, NT):
        got(row.at[(t + k) % NT], R_ROW + k, at_t(k))
    for k in x_all:
        gather_got(lambda i: cf.at[i], R_CF, k)
    for i in range(NT):
        factors = row[i]
        coef = cf[i].astype(F32) * to_col(factors[0:1, 0:nq])
        marks = hot[i]
        coef = jnp.where(marks == 1.0, to_col(factors[1:2, 0:nq]) * inv_d, coef)
        coef = jnp.where(marks == 2.0, to_col(factors[2:3, 0:nq]) * inv_d, coef)
        cg[i] = coef.astype(BF16)

    inner = cg[t].astype(F32) * full[0:nq]
    kz[z] = rows8(pad_lanes(to_row(jnp.sum(inner, axis=1, keepdims=True)), 128))
    kd[t] = rows8(jnp.sum(inner, axis=0, keepdims=True), jnp.broadcast_to(loss_part, (1, all_d)))
    for k in Z_ORDER:
        push(kz.at[z], kz.at[z], R_KZ + 8 - k, at_z(k))
    for k in range(1, NT):
        push(kd.at[t], kd.at[t], R_KD + 8 - k, at_t(k))
    def grad_q(k):
        return dot_nn(cg[(z + k) % NZ], dall[...].reshape(all_d, width))

    for i, k in enumerate((3, 5)):
        sq[i] = grad_q(k).astype(BF16)
        push(sq.at[i], rq1.at[i], R_G1 + i, at_z(1 if k == 3 else 7))
    sq[2] = grad_q(4).astype(BF16)
    push(sq.at[2, halves[2]], rqh.at[0], R_GH, at_z(2))
    push(sq.at[2, halves[6]], rqh.at[1], R_GH + 1, at_z(6))
    all_q = NZ * nq
    ct[...] = cg[...].reshape(all_q, all_d).T.reshape(NY, nd, all_q)
    for k in Y_ORDER:
        sd[k - 1] = dot_nn(ct[(y + k) % NY], qall[...].reshape(all_q, width)).astype(BF16)
        push(sd.at[k - 1], rd.at[3 - k], R_GD + 4 - k, at_y(k))
    for i, k in enumerate((1, 7)):
        sq[3 + i] = grad_q(k).astype(BF16)
        push(sq.at[3 + i], rq.at[1 - i], R_GQ + 8 - k, at_z(k))
    for i, k in enumerate((2, 6)):
        hold[i] = grad_q(k)
    for i, k in enumerate((2, 6)):
        got(rq1.at[i], R_G1 + i, at_z(7 if k == 2 else 1))
        got(rqh.at[i], R_GH + i, at_z(8 - k))
        low = slice(0, half) if k == 2 else slice(half, nq)
        high = slice(half, nq) if k == 2 else slice(0, half)
        summed = hold[i] + rq1[i].astype(F32)
        sq[5 + i, low] = (summed[low] + rqh[i].astype(F32)).astype(BF16)
        sq[5 + i, high] = summed[high].astype(BF16)
        push(sq.at[5 + i], rq.at[3 - i], R_GQ + 8 - k, at_z(k))
    grad_d = dot_nn(ct[y], qall[...].reshape(all_q, width))
    acc[0:nq] = grad_q(0)

    for k in range(1, NT):
        got(kd.at[(t + k) % NT], R_KD + k, at_t(k))
    summed = kd[0]
    for k in range(1, NT):
        summed = summed + kd[k]
    summed = rows8(summed[0:1], summed[1:2], inv_d * inv_d)
    for k in range(NY):
        kds[k] = summed[:, k * nd : (k + 1) * nd]
    for k in Y_ORDER:
        push(kds.at[(y + k) % NY], ky.at[y], R_KY + 4 - k, at_y(k))
    ky[y] = kds[y]
    for k in Z_ORDER:
        got(kz.at[(z + k) % NZ], R_KZ + k, at_z(k))
    summed = kz[0]
    for k in range(1, NZ):
        summed = summed + kz[k]
    kt[t] = rows8(pad_lanes(summed[0:1, 0:nq] * inv_q_row * inv_q_row, 128))
    for k in range(1, NT):
        push(kt.at[t], kt.at[t], R_KT + 8 - k, at_t(k))

    for k in Y_ORDER:
        got(rd.at[k - 1], R_GD + k, at_y(k))
    for k in (1, 2, 3):
        grad_d = grad_d + rd[k - 1].astype(F32)
    for k in Y_ORDER:
        got(ky.at[(y + k) % NY], R_KY + k, at_y(k))
    summed = ky[0] + ky[1] + ky[2] + ky[3]
    loss_out[0, 0] = jnp.sum(summed[1:2, 0:1]) * (1.0 / (NY * NZ * nq))
    inverse2 = kds[y]
    factor = to_col(summed[0:1] * inverse2[2:3])
    gp[t, nq:] = (gain * (grad_d - dall[y].astype(F32) * factor)).astype(BF16)
    gather_start(lambda i: gp.at[i, d_rows], R_PD)

    for i, k in enumerate((1, 7, 2, 6)):
        got(rq.at[i], R_GQ + k, at_z(k))
    for k in range(1, NT):
        got(kt.at[(t + k) % NT], R_KT + k, at_t(k))
    grad = acc[0:nq]
    for i in range(4):
        grad = grad + rq[i].astype(F32)
    factor = kt[z]
    factor = to_col(factor[0:1, 0:nq])
    gp[t, 0:nq] = (gain * (grad - qall[z].astype(F32) * factor)).astype(BF16)
    gather_start(lambda i: gp.at[i, q_rows], R_PQ)

    gather_pass(lambda i: gp.at[i, d_rows], R_PD)
    result = None
    for a in (0, 1):
        for k in (0,) + X_ORDER:
            if a:
                gather_got(lambda i: gp.at[i, d_rows], R_PD, k)
            owner = 2 * ((x + k) % NX) + (c + a) % 2
            term = dot_nn(gp[owner, nq:], wt[4 * a + k])
            result = term if result is None else result + term
    out[nq:] = result.astype(BF16)
    result = None
    for a in (0, 1):
        for k in (0,) + X_ORDER:
            owner = 2 * ((x + k) % NX) + (c + a) % 2
            if a:
                gather_got(lambda i: gp.at[i, q_rows], R_PQ, k)
            elif k:
                slot = gp.at[owner, q_rows]
                got(slot, R_PQ + k, at_x(k))
                push(slot, slot, R_PQ + 4 + k, sib)
            term = dot_nn(gp[owner, 0:nq], wt[4 * a + k])
            result = term if result is None else result + term
    out[0:nq] = result.astype(BF16)
    for copy in sends:
        copy.wait_send()
    for k, copy in passed:

        @pl.when(parity == k % 2)
        def _(copy=copy):
            copy.wait_send()


def shards(
    query_residual, query_hidden, doc_residual, doc_hidden, down_weight, norm_gain, pos_index, neg_index,
):
    nq, width = query_residual.shape
    nd = doc_residual.shape[0]
    depth = query_hidden.shape[1]
    n = nq + nd
    all_q, all_d = NZ * nq, NY * nd
    hbm = pl.BlockSpec(memory_space=pltpu.HBM)
    vmem = pl.BlockSpec(memory_space=pltpu.VMEM)
    grads, loss = pl.pallas_call(
        functools.partial(kernel, nq, nd),
        out_shape=(pltpu.VMEM((n, depth), BF16), jax.ShapeDtypeStruct((1, 1), F32)),
        in_specs=[hbm] * 8,
        out_specs=(vmem, pl.BlockSpec(memory_space=pltpu.SMEM)),
        scratch_shapes=[
            pltpu.VMEM((NT, 1, width), F32),
            pltpu.VMEM((NZ * NY * nq // 128, 1, 128), jnp.int32),
            pltpu.VMEM((NZ * NY * nq // 128, 1, 128), jnp.int32),
            pltpu.VMEM((n, depth), BF16),
            pltpu.VMEM((n, width), BF16),
            pltpu.VMEM((NT, depth, width), BF16),
            pltpu.VMEM((NT, width, depth), BF16),
            pltpu.VMEM((NX, n, width), BF16),
            pltpu.VMEM((NX, n, width), BF16),
            pltpu.VMEM((NX - 1, n, width), BF16),
            pltpu.VMEM((NX - 1, n, width), BF16),
            pltpu.VMEM((n, width), F32),
            pltpu.VMEM((NZ, nq, width), BF16),
            pltpu.VMEM((NZ, nq, width), BF16),
            pltpu.VMEM((NY, nd, width), BF16),
            pltpu.VMEM((NY, nd, width), BF16),
            pltpu.VMEM((NX, nq + 8, all_d), F32),
            pltpu.VMEM((NX - 1, nq + 8, all_d), F32),
            pltpu.VMEM((NZ, 8, 128), F32),
            pltpu.VMEM((NT, 8, 128), F32),
            pltpu.VMEM((NT, nq, all_d), F32),
            pltpu.VMEM((NT, nq, all_d), BF16),
            pltpu.VMEM((NT, nq, all_d), BF16),
            pltpu.VMEM((NY, nd, all_q), BF16),
            pltpu.VMEM((NZ - 1, nq, width), BF16),
            pltpu.VMEM((2, nq, width), F32),
            pltpu.VMEM((2, nq, width), BF16),
            pltpu.VMEM((2, nq // 2, width), BF16),
            pltpu.VMEM((4, nq, width), BF16),
            pltpu.VMEM((NY - 1, nd, width), BF16),
            pltpu.VMEM((NY - 1, nd, width), BF16),
            pltpu.VMEM((NZ, 8, 128), F32),
            pltpu.VMEM((NT, 8, 128), F32),
            pltpu.VMEM((NT, 8, all_d), F32),
            pltpu.VMEM((NY, 8, nd), F32),
            pltpu.VMEM((NY, 8, nd), F32),
            pltpu.VMEM((NT, n, width), BF16),
            pltpu.SemaphoreType.DMA((16,)),
            pltpu.SemaphoreType.DMA((N_SEND,)),
            pltpu.SemaphoreType.DMA((RID.n,)),
        ],
        compiler_params=pltpu.CompilerParams(
            collective_id=0, has_side_effects=True, vmem_limit_bytes=62 * 2**20
        ),
        name="step",
    )(
        query_residual, query_hidden, doc_residual, doc_hidden, down_weight,
        norm_gain.reshape(NT, 1, width), pos_index.reshape(-1, 1, 128), neg_index.reshape(-1, 1, 128),
    )
    return grads[:nq], grads[nq:], loss.reshape(())


def solution(mesh):
    placed = (
        P("dp", "tensor"),
        P("dp", "tensor"),
        P("dp", "tensor"),
        P("dp", "tensor"),
        P("tensor", None),
        P(),
        P(),
        P(),
    )
    return jax.shard_map(
        shards,
        mesh=mesh,
        in_specs=placed,
        out_specs=(P("dp", "tensor"), P("dp", "tensor"), P()),
        check_vma=False,
    )
```

```python
import functools

import jax
import jax.numpy as jnp
from jax import lax
from jax.experimental import pallas as pl
from jax.experimental.pallas import tpu as pltpu
from jax.sharding import PartitionSpec as P

EPS = 1e-06
TAU = 0.05
LOSS_SCALE = 256.0
NX, NY, NZ = 4, 4, 8
NT = 2 * NX
MESH = pl.DeviceIdType.MESH
F32 = jnp.float32
BF16 = jnp.bfloat16


def dot_nn(a, b):
    return lax.dot_general(a, b, (((1,), (0,)), ((), ())), preferred_element_type=F32)


def dot_nt(a, b):
    return lax.dot_general(a, b, (((1,), (1,)), ((), ())), preferred_element_type=F32)


def eye(n, m, shift=0):
    rows = lax.broadcasted_iota(jnp.int32, (n, m), 0)
    cols = lax.broadcasted_iota(jnp.int32, (n, m), 1)
    return cols == rows + shift


def to_row(col):
    n = col.shape[0]
    return jnp.sum(jnp.where(eye(n, n), col, 0.0), axis=0, keepdims=True)


def to_col(row):
    n = row.shape[1]
    return jnp.sum(jnp.where(eye(n, n), row, 0.0), axis=1, keepdims=True)


def rows8(*rows):
    width = rows[0].shape[1]
    index = lax.broadcasted_iota(jnp.int32, (8, width), 0)
    out = jnp.zeros((8, width), F32)
    for i, row in enumerate(rows):
        out = jnp.where(index == i, row, out)
    return out


def pad_lanes(row, width):
    return jnp.concatenate([row, jnp.zeros((1, width - row.shape[1]), F32)], axis=1)


class Ids:
    def __init__(self):
        self.n = 0

    def take(self, n):
        base = self.n
        self.n += n
        return base


RID = Ids()
R_SIB = RID.take(4)
R_XQ, R_XD = RID.take(1), (RID.take(1), RID.take(1))
R_Z2, R_Z6, R_Z1, R_Z3, R_QS = (RID.take(1) for _ in range(5))
R_YD, R_DS = (RID.take(1), RID.take(1)), RID.take(1)
R_SX, R_SS = RID.take(1), RID.take(1)
R_STAT, R_ROW = RID.take(1), RID.take(1)
R_CF, R_CS = RID.take(4), RID.take(1)
R_G1, R_GH, R_GQ = RID.take(2), RID.take(2), RID.take(1)
R_GD = (RID.take(1), RID.take(1))
R_KZ, R_KT, R_KD, R_KY = (RID.take(1) for _ in range(4))
R_PD, R_PDS, R_PQ, R_PQS = (RID.take(1), RID.take(1)), RID.take(1), RID.take(4), RID.take(1)
X_ORDER = (2, 1, 3)
Z_ORDER = (4, 3, 5, 2, 6, 1, 7)
Y_ORDER = (2, 1, 3)


def kernel(
    nq, nd, q_res, q_hid, d_res, d_hid, w_hbm, gain_hbm, pos_hbm, neg_hbm,
    out, loss_out,
    gain_ref, pos_ref, neg_ref, hid, res, wv, wt, s1, r1, s2, r2, acc, qall, qs, dall, ds, s3, r3, s3t, r3t, stats,
    row, hot, cf, cg, ct, sq, hold, rq1, rqh, rq, sd, rd, kz, kt, kd, kds, ky, gp, local, send, recv,
):
    dp = lax.axis_index("dp")
    t = lax.axis_index("tensor")
    x, c = t // 2, t % 2
    y, z = dp // NZ, dp % NZ

    def at_x(k):
        return (dp, 2 * ((x + k) % NX) + c)

    def at_t(k):
        return (dp, (t + k) % NT)

    def at_y(k):
        return (((y + k) % NY) * NZ + z, t)

    def at_z(k):
        return (y * NZ + (z + k) % NZ, t)

    sib = (dp, 2 * x + 1 - c)
    sends = []

    def push(src, dst, rid, device):
        copy = pltpu.make_async_remote_copy(
            src_ref=src, dst_ref=dst, send_sem=send.at[0], recv_sem=recv.at[rid],
            device_id=device, device_id_type=MESH,
        )
        copy.start()
        sends.append(copy)

    def got(dst, rid, device):
        pltpu.make_async_remote_copy(
            src_ref=dst, dst_ref=dst, send_sem=send.at[0], recv_sem=recv.at[rid],
            device_id=device, device_id_type=MESH,
        ).wait_recv()

    def turn(first, last):
        for i in range(first, last):
            wt[i] = wv[i].T

    loads = []

    def load(src, dst):
        copy = pltpu.make_async_copy(src, dst, local.at[len(loads)])
        copy.start()
        loads.append(copy)
        return copy

    h_loads = [load(q_hid, hid.at[pl.ds(0, nq)]), load(d_hid, hid.at[pl.ds(nq, nd)])]
    x_all = X_ORDER + (0,)
    w_loads = {}
    width = res.shape[1]
    steps = ((1, 2), (1, 1), (0, 2), (1, 3), (0, 1), (1, 0), (0, 3), (0, 0))
    for a, k in steps:
        owner = 2 * ((x + k) % NX) + (c + a) % 2
        columns = pl.ds(pl.multiple_of(owner * width, width), width)
        w_loads[a, k] = load(w_hbm.at[:, columns], wv.at[4 * a + k])
    r_loads = [load(gain_hbm, gain_ref), load(pos_hbm, pos_ref), load(neg_hbm, neg_ref)]
    r_loads += [load(q_res, res.at[pl.ds(0, nq)]), load(d_res, res.at[pl.ds(nq, nd)])]

    barrier = pltpu.get_barrier_semaphore()
    peers = [at_t(k) for k in range(1, NT)] + [at_z(k) for k in range(1, NZ)]
    peers += [at_y(k) for k in range(1, NY)]
    for peer in peers:
        pl.semaphore_signal(barrier, inc=1, device_id=peer, device_id_type=MESH)

    for copy in h_loads:
        copy.wait()
    q_rows, d_rows = pl.ds(0, nq), pl.ds(nq, nd)
    d_parts = [pl.ds(nq + i * (nd // 2), nd // 2) for i in range(2)]
    for i, (a, k) in enumerate(steps):
        w_loads[a, k].wait()
        part = dot_nn(hid[...], wv[4 * a + k])
        if a:
            s1[k] = part.astype(BF16)
            if i == 0:
                pl.semaphore_wait(barrier, len(peers))
            push(s1.at[k], r1.at[k], R_SIB + k, sib)
            continue
        got(r1.at[k], R_SIB + k, sib)
        part = part + r1[k].astype(F32)
        if k:
            s2[k - 1] = part.astype(BF16)
            push(s2.at[k - 1, q_rows], r2.at[3 - k, q_rows], R_XQ, at_x(k))
            push(s2.at[k - 1, d_parts[0]], r2.at[3 - k, d_parts[0]], R_XD[0], at_x(k))
        else:
            acc[...] = part
        if k == 3:
            for k in X_ORDER:
                push(s2.at[k - 1, d_parts[1]], r2.at[3 - k, d_parts[1]], R_XD[1], at_x(k))
    for copy in r_loads:
        copy.wait()
    gain = gain_ref[t]

    parity = (z + c + 1) % 2
    passed = []

    def pass_q(k):
        slot = (z + k) % NZ
        copy = pltpu.make_async_remote_copy(
            src_ref=qall.at[slot], dst_ref=qs.at[slot], send_sem=send.at[0],
            recv_sem=recv.at[R_QS], device_id=sib, device_id_type=MESH,
        )
        passed.append((k, copy))

        @pl.when(parity == k % 2)
        def _():
            copy.start()

    def full_rows(rows):
        total = acc[rows] + res[rows].astype(F32)
        for k in (1, 2, 3):
            total = total + r2[k - 1, rows].astype(F32)
        return (total * gain).astype(BF16)

    got(r2.at[:, q_rows], R_XQ, sib)
    qall[z] = full_rows(slice(0, nq))
    for k in (2, 6, 1, 7):
        push(qall.at[z], qall.at[z], {2: R_Z6, 6: R_Z2}.get(k, R_Z1), at_z(k))
    pass_q(0)
    turn(0, 2)
    for i in range(2):
        got(r2.at[:, d_parts[i]], R_XD[i], sib)
        low = i * (nd // 2)
        dall[y, low : low + nd // 2] = full_rows(slice(nq + low, nq + low + nd // 2))
        slot = dall.at[y, pl.ds(low, nd // 2)]
        for k in Y_ORDER:
            push(slot, slot, R_YD[i], at_y(k))
        push(slot, ds.at[y, pl.ds(low, nd // 2)], R_DS, sib)
    half = nq // 2
    halves = {2: pl.ds(0, half), 6: pl.ds(half, half)}
    for k in (2, 6):
        slot = (z + k) % NZ
        got(qall.at[slot], R_Z2 if k == 2 else R_Z6, at_z(k))
        push(qall.at[slot], qall.at[slot], R_Z3, at_z(7 if k == 2 else 1))
        part = qall.at[slot, halves[k]]
        push(part, part, R_Z3, at_z(8 - k))
        pass_q(k)
    got(qall.at[pl.ds(0, 2)], R_Z1, sib)
    pass_q(1)
    pass_q(7)
    all_d = NY * nd
    lanes = lax.broadcasted_iota(jnp.int32, (1, all_d), 1)
    column = ((lanes // nd) * NZ + z) * nd + lanes % nd
    for i in range(NZ):
        at = y * (NZ * nq // 128) + i * nq // 128
        pick = eye(nq, 128, i * nq % 128)
        pos = jnp.sum(jnp.where(pick, pos_ref[at].astype(F32), 0.0), axis=1, keepdims=True)
        neg = jnp.sum(jnp.where(pick, neg_ref[at].astype(F32), 0.0), axis=1, keepdims=True)
        mark = jnp.where(column == neg.astype(jnp.int32), 2.0, 0.0)
        hot[i] = jnp.where(column == pos.astype(jnp.int32), 1.0, mark)
    turn(2, 4)

    for i in range(2):
        place = pl.ds(i * (nd // 2), nd // 2)
        got(dall.at[pl.ds(0, 3), place], R_YD[i], sib)
        for k in Y_ORDER:
            slot = (y + k) % NY
            push(dall.at[slot, place], ds.at[slot, place], R_DS, sib)
    got(qall.at[pl.ds(0, 3)], R_Z3, sib)
    for k in (3, 5, 4):
        pass_q(k)

    got(ds, R_DS, sib)

    def squares(*blocks):
        total = 0.0
        for rows in blocks:
            wide = rows.astype(F32)
            total = total + wide * wide
        return to_row(jnp.sum(total, axis=1, keepdims=True))

    ss_d = jnp.concatenate([squares(dall[k], ds[k]) for k in range(NY)], axis=1)
    got(qs.at[pl.ds(0, NZ // 2)], R_QS, sib)
    owners = [2 * ((x + k) % NX) + c for k in x_all]
    for k, owner in zip(x_all, owners):
        s3t[k] = rows8(pad_lanes(squares(qall[owner], qs[owner]), all_d), ss_d)
        if k:
            push(s3t.at[k], r3t.at[3 - k], R_SS, at_x(k))
    scores = dot_nt(jnp.concatenate([qall[i] for i in owners], 0), dall[...].reshape(all_d, width))
    scores = scores + dot_nt(jnp.concatenate([qs[i] for i in owners], 0), ds[...].reshape(all_d, width))
    for i, k in enumerate(X_ORDER):
        s3[k - 1] = scores[i * nq : (i + 1) * nq].astype(BF16)
        push(s3.at[k - 1], r3.at[3 - k], R_SX, at_x(k))
    own_scores = scores[3 * nq :]
    turn(4, 6)
    got(r3t, R_SS, sib)
    tail = s3t[0] + r3t[0] + r3t[1] + r3t[2]
    inv_d = lax.rsqrt(tail[1:2] + EPS)
    inv_q_row = lax.rsqrt(tail[0:1, 0:nq] + EPS)
    inv_q = to_col(inv_q_row)
    got(r3, R_SX, sib)
    full = own_scores
    for k in (1, 2, 3):
        full = full + r3[k - 1].astype(F32)

    scores = full * inv_q * inv_d * (1.0 / TAU)
    expo = jnp.exp(scores)
    marks = hot[t]
    pos_hot, neg_hot = marks == 1.0, marks == 2.0
    stats[z] = rows8(
        pad_lanes(to_row(jnp.sum(expo, axis=1, keepdims=True)), 128),
        pad_lanes(to_row(jnp.sum(jnp.where(pos_hot, scores, 0.0), axis=1, keepdims=True)), 128),
        pad_lanes(to_row(jnp.sum(jnp.where(neg_hot, scores, 0.0), axis=1, keepdims=True)), 128),
    )
    def gather_start(ref, rid, pass_rid, each=1):
        for k in X_ORDER:
            push(ref(t), ref(t), rid + each * (4 - k), at_x(k))
        push(ref(t), ref(t), pass_rid, sib)

    def gather_pass(ref, pass_rid, k):
        slot = ref(2 * ((x + k) % NX) + c)
        push(slot, slot, pass_rid, sib)

    for k in Z_ORDER:
        push(stats.at[z], stats.at[z], R_STAT, at_z(k))
    cf[t] = (expo * inv_d).astype(BF16)
    gather_start(lambda i: cf.at[i], R_CF, R_CS)
    turn(6, 8)
    got(stats.at[pl.ds(0, NZ - 1)], R_STAT, sib)
    stat = stats[0]
    for k in range(1, NZ):
        stat = stat + stats[k]
    tot_row, pos_row, neg_row = stat[0:1, 0:nq], stat[1:2, 0:nq], stat[2:3, 0:nq]
    margin = neg_row - pos_row
    low = jnp.exp(-jnp.abs(margin))
    sig = jnp.where(margin >= 0.0, 1.0, low) / (1.0 + low)
    scale = (LOSS_SCALE / TAU) * inv_q_row
    row[t] = rows8(
        pad_lanes(scale / tot_row, 128),
        pad_lanes(scale * (jnp.exp(pos_row) / tot_row - (1.0 + sig)), 128),
        pad_lanes(scale * (jnp.exp(neg_row) / tot_row + sig), 128),
    )
    for k in range(1, NT):
        push(row.at[t], row.at[t], R_ROW, at_t(k))
    soft = jnp.maximum(margin, 0.0) + jnp.log1p(low)
    loss_part = jnp.sum(jnp.log(tot_row) - pos_row + soft, axis=1, keepdims=True)
    for k in X_ORDER:
        got(cf.at[2 * ((x + k) % NX) + c], R_CF + k, at_x(k))
        gather_pass(lambda i: cf.at[i], R_CS, k)
    got(row.at[pl.ds(0, NT - 1)], R_ROW, sib)
    got(cf.at[pl.ds(0, NX)], R_CS, sib)
    for i in range(NT):
        factors = row[i]
        coef = cf[i].astype(F32) * to_col(factors[0:1, 0:nq])
        marks = hot[i]
        coef = jnp.where(marks == 1.0, to_col(factors[1:2, 0:nq]) * inv_d, coef)
        coef = jnp.where(marks == 2.0, to_col(factors[2:3, 0:nq]) * inv_d, coef)
        cg[i] = coef.astype(BF16)

    inner = cg[t].astype(F32) * full
    kz[z] = rows8(pad_lanes(to_row(jnp.sum(inner, axis=1, keepdims=True)), 128))
    kd[t] = rows8(jnp.sum(inner, axis=0, keepdims=True), jnp.broadcast_to(loss_part, (1, all_d)))
    for k in Z_ORDER:
        push(kz.at[z], kz.at[z], R_KZ, at_z(k))
    for k in range(1, NT):
        push(kd.at[t], kd.at[t], R_KD, at_t(k))
    def grad_q(*offsets):
        rows = [cg[(z + k) % NZ] for k in offsets]
        grad = dot_nn(jnp.concatenate(rows, 0), dall[...].reshape(all_d, width))
        return [grad[i * nq : (i + 1) * nq] for i in range(len(offsets))]

    for i, grad in enumerate(grad_q(3, 5, 4)):
        sq[i] = grad.astype(BF16)
    for i, k in enumerate((3, 5)):
        push(sq.at[i], rq1.at[i], R_G1 + i, at_z(1 if k == 3 else 7))
    push(sq.at[2, halves[2]], rqh.at[0], R_GH, at_z(2))
    push(sq.at[2, halves[6]], rqh.at[1], R_GH + 1, at_z(6))
    all_q = NZ * nq
    ct[...] = cg[...].reshape(all_q, all_d).T.reshape(NY, nd, all_q)
    rows = jnp.concatenate([ct[(y + k) % NY] for k in Y_ORDER + (0,)], 0)
    grad = dot_nn(rows, qall[...].reshape(all_q, width))
    d_halves = [pl.ds(i * (nd // 2), nd // 2) for i in range(2)]
    for i, k in enumerate(Y_ORDER):
        sd[k - 1] = grad[i * nd : (i + 1) * nd].astype(BF16)
    acc[nq:] = grad[3 * nd :]
    for half_at, rid in zip(d_halves, R_GD):
        for k in Y_ORDER:
            push(sd.at[k - 1, half_at], rd.at[3 - k, half_at], rid, at_y(k))
    first, second, third, fourth, own = grad_q(1, 7, 2, 6, 0)
    sq[3], sq[4] = first.astype(BF16), second.astype(BF16)
    for i, k in enumerate((1, 7)):
        push(sq.at[3 + i], rq.at[1 - i], R_GQ, at_z(k))
    hold[0], hold[1] = third, fourth
    acc[0:nq] = own
    got(kd.at[pl.ds(0, NT - 1)], R_KD, sib)
    summed = kd[0]
    for k in range(1, NT):
        summed = summed + kd[k]
    summed = rows8(summed[0:1], summed[1:2], inv_d * inv_d)
    for k in range(NY):
        kds[k] = summed[:, k * nd : (k + 1) * nd]
    for k in Y_ORDER:
        push(kds.at[(y + k) % NY], ky.at[y], R_KY, at_y(k))
    ky[y] = kds[y]
    for i, k in enumerate((2, 6)):
        got(rq1.at[i], R_G1 + i, at_z(7 if k == 2 else 1))
        got(rqh.at[i], R_GH + i, at_z(8 - k))
        low = slice(0, half) if k == 2 else slice(half, nq)
        high = slice(half, nq) if k == 2 else slice(0, half)
        summed = hold[i] + rq1[i].astype(F32)
        sq[5 + i, low] = (summed[low] + rqh[i].astype(F32)).astype(BF16)
        sq[5 + i, high] = summed[high].astype(BF16)
        push(sq.at[5 + i], rq.at[3 - i], R_GQ, at_z(k))
    got(kz.at[pl.ds(0, NZ - 1)], R_KZ, sib)
    summed = kz[0]
    for k in range(1, NZ):
        summed = summed + kz[k]
    kt[t] = rows8(pad_lanes(summed[0:1, 0:nq] * inv_q_row * inv_q_row, 128))
    for k in range(1, NT):
        push(kt.at[t], kt.at[t], R_KT, at_t(k))

    got(ky.at[pl.ds(0, NY - 1)], R_KY, sib)
    summed = ky[0] + ky[1] + ky[2] + ky[3]
    loss_out[0, 0] = jnp.sum(summed[1:2, 0:1]) * (1.0 / (NY * NZ * nq))
    inverse2 = kds[y]
    factor = to_col(summed[0:1] * inverse2[2:3])
    for i in range(2):
        low, high = i * (nd // 2), (i + 1) * (nd // 2)
        got(rd.at[:, d_halves[i]], R_GD[i], sib)
        grad = acc[nq + low : nq + high]
        for k in (1, 2, 3):
            grad = grad + rd[k - 1, low:high].astype(F32)
        pre = gain * (grad - dall[y, low:high].astype(F32) * factor[low:high])
        gp[t, nq + low : nq + high] = pre.astype(BF16)
        gather_start(lambda j, i=i: gp.at[j, d_parts[i]], R_PD[i], R_PDS, 0)

    got(rq, R_GQ, sib)
    got(kt.at[pl.ds(0, NT - 1)], R_KT, sib)
    grad = acc[0:nq]
    for i in range(4):
        grad = grad + rq[i].astype(F32)
    factor = kt[z]
    factor = to_col(factor[0:1, 0:nq])
    gp[t, 0:nq] = (gain * (grad - qall[z].astype(F32) * factor)).astype(BF16)
    gather_start(lambda j: gp.at[j, q_rows], R_PQ, R_PQS)

    for i in range(2):
        got(gp.at[pl.ds(0, 3), d_parts[i]], R_PD[i], sib)
        for k in X_ORDER:
            gather_pass(lambda j, i=i: gp.at[j, d_parts[i]], R_PDS, k)
    result = None
    for a in (0, 1):
        if a:
            got(gp.at[pl.ds(0, NX), d_rows], R_PDS, sib)
        for k in (0,) + X_ORDER:
            owner = 2 * ((x + k) % NX) + (c + a) % 2
            term = dot_nn(gp[owner, nq:], wt[4 * a + k])
            result = term if result is None else result + term
    out[nq:] = result.astype(BF16)
    result = None
    for a in (0, 1):
        if a:
            got(gp.at[pl.ds(0, NX), q_rows], R_PQS, sib)
        for k in (0,) + X_ORDER:
            owner = 2 * ((x + k) % NX) + (c + a) % 2
            if k and not a:
                got(gp.at[owner, q_rows], R_PQ + k, at_x(k))
                gather_pass(lambda j: gp.at[j, q_rows], R_PQS, k)
            term = dot_nn(gp[owner, 0:nq], wt[4 * a + k])
            result = term if result is None else result + term
    out[0:nq] = result.astype(BF16)
    for copy in sends:
        copy.wait_send()
    for k, copy in passed:

        @pl.when(parity == k % 2)
        def _(copy=copy):
            copy.wait_send()


def shards(
    query_residual, query_hidden, doc_residual, doc_hidden, down_weight, norm_gain, pos_index, neg_index,
):
    nq, width = query_residual.shape
    nd = doc_residual.shape[0]
    depth = query_hidden.shape[1]
    n = nq + nd
    all_q, all_d = NZ * nq, NY * nd
    hbm = pl.BlockSpec(memory_space=pltpu.HBM)
    vmem = pl.BlockSpec(memory_space=pltpu.VMEM)
    grads, loss = pl.pallas_call(
        functools.partial(kernel, nq, nd),
        out_shape=(pltpu.VMEM((n, depth), BF16), jax.ShapeDtypeStruct((1, 1), F32)),
        in_specs=[hbm] * 8,
        out_specs=(vmem, pl.BlockSpec(memory_space=pltpu.SMEM)),
        scratch_shapes=[
            pltpu.VMEM((NT, 1, width), F32),
            pltpu.VMEM((NZ * NY * nq // 128, 1, 128), jnp.int32),
            pltpu.VMEM((NZ * NY * nq // 128, 1, 128), jnp.int32),
            pltpu.VMEM((n, depth), BF16),
            pltpu.VMEM((n, width), BF16),
            pltpu.VMEM((NT, depth, width), BF16),
            pltpu.VMEM((NT, width, depth), BF16),
            pltpu.VMEM((NX, n, width), BF16),
            pltpu.VMEM((NX, n, width), BF16),
            pltpu.VMEM((NX - 1, n, width), BF16),
            pltpu.VMEM((NX - 1, n, width), BF16),
            pltpu.VMEM((n, width), F32),
            pltpu.VMEM((NZ, nq, width), BF16),
            pltpu.VMEM((NZ, nq, width), BF16),
            pltpu.VMEM((NY, nd, width), BF16),
            pltpu.VMEM((NY, nd, width), BF16),
            pltpu.VMEM((NX - 1, nq, all_d), BF16),
            pltpu.VMEM((NX - 1, nq, all_d), BF16),
            pltpu.VMEM((NX, 8, all_d), F32),
            pltpu.VMEM((NX - 1, 8, all_d), F32),
            pltpu.VMEM((NZ, 8, 128), F32),
            pltpu.VMEM((NT, 8, 128), F32),
            pltpu.VMEM((NT, nq, all_d), F32),
            pltpu.VMEM((NT, nq, all_d), BF16),
            pltpu.VMEM((NT, nq, all_d), BF16),
            pltpu.VMEM((NY, nd, all_q), BF16),
            pltpu.VMEM((NZ - 1, nq, width), BF16),
            pltpu.VMEM((2, nq, width), F32),
            pltpu.VMEM((2, nq, width), BF16),
            pltpu.VMEM((2, nq // 2, width), BF16),
            pltpu.VMEM((4, nq, width), BF16),
            pltpu.VMEM((NY - 1, nd, width), BF16),
            pltpu.VMEM((NY - 1, nd, width), BF16),
            pltpu.VMEM((NZ, 8, 128), F32),
            pltpu.VMEM((NT, 8, 128), F32),
            pltpu.VMEM((NT, 8, all_d), F32),
            pltpu.VMEM((NY, 8, nd), F32),
            pltpu.VMEM((NY, 8, nd), F32),
            pltpu.VMEM((NT, n, width), BF16),
            pltpu.SemaphoreType.DMA((16,)),
            pltpu.SemaphoreType.DMA((1,)),
            pltpu.SemaphoreType.DMA((RID.n,)),
        ],
        compiler_params=pltpu.CompilerParams(
            collective_id=0, has_side_effects=True, vmem_limit_bytes=62 * 2**20
        ),
        name="step",
    )(
        query_residual, query_hidden, doc_residual, doc_hidden, down_weight,
        norm_gain.reshape(NT, 1, width), pos_index.reshape(-1, 1, 128), neg_index.reshape(-1, 1, 128),
    )
    return grads[:nq], grads[nq:], loss.reshape(())


def solution(mesh):
    placed = (
        P("dp", "tensor"),
        P("dp", "tensor"),
        P("dp", "tensor"),
        P("dp", "tensor"),
        P("tensor", None),
        P(),
        P(),
        P(),
    )
    return jax.shard_map(
        shards,
        mesh=mesh,
        in_specs=placed,
        out_specs=(P("dp", "tensor"), P("dp", "tensor"), P()),
        check_vma=False,
    )
```

```python
import functools
import math

import jax
import jax.numpy as jnp
from jax import lax
from jax.experimental import pallas as pl
from jax.experimental.pallas import tpu as pltpu
from jax.sharding import PartitionSpec as P

EPS = 1e-06
TAU = 0.05
LOSS_SCALE = 256.0
NX, NY, NZ = 4, 4, 8
NT = 2 * NX
MESH = pl.DeviceIdType.MESH
F32 = jnp.float32
BF16 = jnp.bfloat16


def dot_nn(a, b):
    return lax.dot_general(a, b, (((1,), (0,)), ((), ())), preferred_element_type=F32)


def dot_nt(a, b):
    return lax.dot_general(a, b, (((1,), (1,)), ((), ())), preferred_element_type=F32)


def eye(n, m, shift=0):
    rows = lax.broadcasted_iota(jnp.int32, (n, m), 0)
    cols = lax.broadcasted_iota(jnp.int32, (n, m), 1)
    return cols == rows + shift


def to_row(col):
    n = col.shape[0]
    return jnp.sum(jnp.where(eye(n, n), col, 0.0), axis=0, keepdims=True)


def to_col(row):
    n = row.shape[1]
    return jnp.sum(jnp.where(eye(n, n), row, 0.0), axis=1, keepdims=True)


def rows8(*rows):
    width = rows[0].shape[1]
    index = lax.broadcasted_iota(jnp.int32, (8, width), 0)
    out = jnp.zeros((8, width), F32)
    for i, row in enumerate(rows):
        out = jnp.where(index == i, row, out)
    return out


def pad_lanes(row, width):
    return jnp.concatenate([row, jnp.zeros((1, width - row.shape[1]), F32)], axis=1)


class Ids:
    def __init__(self):
        self.n = 0

    def take(self, n):
        base = self.n
        self.n += n
        return base


RID = Ids()
R_SIB = RID.take(4)
R_XQ, R_XD = RID.take(1), (RID.take(1), RID.take(1))
R_Z2, R_Z6, R_Z1, R_Z3, R_QS = (RID.take(1) for _ in range(5))
R_YD, R_DS = (RID.take(1), RID.take(1)), RID.take(1)
R_SX, R_SS = RID.take(1), RID.take(1)
R_STAT, R_ROW = RID.take(1), RID.take(1)
R_CF, R_CS = RID.take(4), RID.take(1)
R_G1, R_GH, R_GQ = RID.take(2), RID.take(2), RID.take(1)
R_GD = (RID.take(1), RID.take(1))
R_KZ, R_KT, R_KD, R_KY = (RID.take(1) for _ in range(4))
R_PD, R_PDS, R_PQ, R_PQS = (RID.take(1), RID.take(1)), RID.take(1), RID.take(4), RID.take(1)
X_ORDER = (2, 1, 3)
Z_ORDER = (4, 3, 5, 2, 6, 1, 7)
Y_ORDER = (2, 1, 3)


def kernel(
    nq, nd, q_res, q_hid, d_res, d_hid, w_hbm, gain_hbm, pos_hbm, neg_hbm,
    out, loss_out,
    gain_ref, pos_ref, neg_ref, hid, res, wv, wt, s1, r1, s2, r2, acc, qall, qs, dall, ds, s3, r3, s3t, r3t, stats,
    row, hot, cf, cg, ct, sq, hold, rq1, rqh, rq, sd, rd, kz, kt, kd, kds, ky, gp, local, send, recv,
):
    dp = lax.axis_index("dp")
    t = lax.axis_index("tensor")
    x, c = t // 2, t % 2
    y, z = dp // NZ, dp % NZ

    def at_x(k):
        return (dp, 2 * ((x + k) % NX) + c)

    def at_t(k):
        return (dp, (t + k) % NT)

    def at_y(k):
        return (((y + k) % NY) * NZ + z, t)

    def at_z(k):
        return (y * NZ + (z + k) % NZ, t)

    sib = (dp, 2 * x + 1 - c)
    sends = []

    def push(src, dst, rid, device):
        copy = pltpu.make_async_remote_copy(
            src_ref=src, dst_ref=dst, send_sem=send.at[0], recv_sem=recv.at[rid],
            device_id=device, device_id_type=MESH,
        )
        copy.start()
        sends.append(math.prod(src.shape) * jnp.dtype(src.dtype).itemsize)

    def got(dst, rid, device):
        pltpu.make_async_remote_copy(
            src_ref=dst, dst_ref=dst, send_sem=send.at[0], recv_sem=recv.at[rid],
            device_id=device, device_id_type=MESH,
        ).wait_recv()

    def turn(first, last):
        for i in range(first, last):
            wt[i] = wv[i].T

    loads = []

    def load(src, dst):
        copy = pltpu.make_async_copy(src, dst, local.at[len(loads)])
        copy.start()
        loads.append(copy)
        return copy

    h_loads = [load(q_hid, hid.at[pl.ds(0, nq)]), load(d_hid, hid.at[pl.ds(nq, nd)])]
    x_all = X_ORDER + (0,)
    w_loads = {}
    depth, width = hid.shape[1], res.shape[1]
    steps = ((1, 2), (1, 1), (0, 2), (1, 3), (0, 1), (1, 0), (0, 3), (0, 0))
    for a, k in steps:
        owner = 2 * ((x + k) % NX) + (c + a) % 2
        columns = pl.ds(pl.multiple_of(owner * width, width), width)
        w_loads[a, k] = load(w_hbm.at[:, columns], wv.at[4 * a + k])
    r_loads = [load(gain_hbm, gain_ref), load(pos_hbm, pos_ref), load(neg_hbm, neg_ref)]
    r_loads += [load(q_res, res.at[pl.ds(0, nq)]), load(d_res, res.at[pl.ds(nq, nd)])]

    barrier = pltpu.get_barrier_semaphore()
    peers = [at_t(k) for k in range(1, NT)] + [at_z(k) for k in range(1, NZ)]
    peers += [at_y(k) for k in range(1, NY)]
    for peer in peers:
        pl.semaphore_signal(barrier, inc=1, device_id=peer, device_id_type=MESH)

    for copy in h_loads:
        copy.wait()
    q_rows, d_rows = pl.ds(0, nq), pl.ds(nq, nd)
    d_parts = [pl.ds(nq + i * (nd // 2), nd // 2) for i in range(2)]
    for i, (a, k) in enumerate(steps):
        w_loads[a, k].wait()
        part = dot_nn(hid[...], wv[4 * a + k])
        if a:
            s1[k] = part.astype(BF16)
            if i == 0:
                pl.semaphore_wait(barrier, len(peers))
            push(s1.at[k], r1.at[k], R_SIB + k, sib)
            continue
        got(r1.at[k], R_SIB + k, sib)
        part = part + r1[k].astype(F32)
        if k:
            s2[k - 1] = part.astype(BF16)
            push(s2.at[k - 1, q_rows], r2.at[3 - k, q_rows], R_XQ, at_x(k))
        else:
            acc[...] = part
        if k == 3:
            for place, rid in zip(d_parts, R_XD):
                for k in X_ORDER:
                    push(s2.at[k - 1, place], r2.at[3 - k, place], rid, at_x(k))
    for copy in r_loads:
        copy.wait()
    gain = gain_ref[t]

    parity = (z + c + 1) % 2

    def pass_q(k):
        slot = (z + k) % NZ
        copy = pltpu.make_async_remote_copy(
            src_ref=qall.at[slot], dst_ref=qs.at[slot], send_sem=send.at[0],
            recv_sem=recv.at[R_QS], device_id=sib, device_id_type=MESH,
        )

        @pl.when(parity == k % 2)
        def _():
            copy.start()

    def full_rows(rows):
        total = acc[rows] + res[rows].astype(F32)
        for k in (1, 2, 3):
            total = total + r2[k - 1, rows].astype(F32)
        return (total * gain).astype(BF16)

    got(r2.at[:, q_rows], R_XQ, sib)
    qall[z] = full_rows(slice(0, nq))
    for k in (2, 6, 1, 7):
        push(qall.at[z], qall.at[z], {2: R_Z6, 6: R_Z2}.get(k, R_Z1), at_z(k))
    pass_q(0)
    turn(0, 2)
    for i in range(2):
        got(r2.at[:, d_parts[i]], R_XD[i], sib)
        low = i * (nd // 2)
        dall[y, low : low + nd // 2] = full_rows(slice(nq + low, nq + low + nd // 2))
        slot = dall.at[y, pl.ds(low, nd // 2)]
        for k in Y_ORDER:
            push(slot, slot, R_YD[i], at_y(k))
        push(slot, ds.at[y, pl.ds(low, nd // 2)], R_DS, sib)
    half = nq // 2
    halves = {2: pl.ds(0, half), 6: pl.ds(half, half)}
    for k in (2, 6):
        slot = (z + k) % NZ
        got(qall.at[slot], R_Z2 if k == 2 else R_Z6, at_z(k))
        push(qall.at[slot], qall.at[slot], R_Z3, at_z(7 if k == 2 else 1))
        part = qall.at[slot, halves[k]]
        push(part, part, R_Z3, at_z(8 - k))
        pass_q(k)
    got(qall.at[pl.ds(0, 2)], R_Z1, sib)
    pass_q(1)
    pass_q(7)
    all_d = NY * nd
    lanes = lax.broadcasted_iota(jnp.int32, (1, all_d), 1)
    column = ((lanes // nd) * NZ + z) * nd + lanes % nd
    for i in range(NZ):
        at = y * (NZ * nq // 128) + i * nq // 128
        pick = eye(nq, 128, i * nq % 128)
        pos = jnp.sum(jnp.where(pick, pos_ref[at].astype(F32), 0.0), axis=1, keepdims=True)
        neg = jnp.sum(jnp.where(pick, neg_ref[at].astype(F32), 0.0), axis=1, keepdims=True)
        mark = jnp.where(column == neg.astype(jnp.int32), 2.0, 0.0)
        hot[i] = jnp.where(column == pos.astype(jnp.int32), 1.0, mark)
    turn(2, 4)

    for i in range(2):
        place = pl.ds(i * (nd // 2), nd // 2)
        got(dall.at[pl.ds(0, 3), place], R_YD[i], sib)
        for k in Y_ORDER:
            slot = (y + k) % NY
            push(dall.at[slot, place], ds.at[slot, place], R_DS, sib)
    got(qall.at[pl.ds(0, 3)], R_Z3, sib)
    for k in (3, 5, 4):
        pass_q(k)

    got(ds, R_DS, sib)

    def squares(*blocks):
        total = 0.0
        for rows in blocks:
            wide = rows.astype(F32)
            total = total + wide * wide
        return to_row(jnp.sum(total, axis=1, keepdims=True))

    got(qs.at[pl.ds(0, NZ // 2)], R_QS, sib)
    owners = [2 * ((x + k) % NX) + c for k in x_all]
    scores = dot_nt(jnp.concatenate([qall[i] for i in owners], 0), dall[...].reshape(all_d, width))
    scores = scores + dot_nt(jnp.concatenate([qs[i] for i in owners], 0), ds[...].reshape(all_d, width))
    for i, k in enumerate(X_ORDER):
        s3[k - 1] = scores[i * nq : (i + 1) * nq].astype(BF16)
        push(s3.at[k - 1], r3.at[3 - k], R_SX, at_x(k))
    own_scores = scores[3 * nq :]
    ss_d = jnp.concatenate([squares(dall[k], ds[k]) for k in range(NY)], axis=1)
    for k, owner in zip(x_all, owners):
        s3t[k] = rows8(pad_lanes(squares(qall[owner], qs[owner]), all_d), ss_d)
        if k:
            push(s3t.at[k], r3t.at[3 - k], R_SS, at_x(k))
    turn(4, 6)
    got(r3t, R_SS, sib)
    tail = s3t[0] + r3t[0] + r3t[1] + r3t[2]
    inv_d = lax.rsqrt(tail[1:2] + EPS)
    inv_q_row = lax.rsqrt(tail[0:1, 0:nq] + EPS)
    inv_q = to_col(inv_q_row)
    got(r3, R_SX, sib)
    full = own_scores
    for k in (1, 2, 3):
        full = full + r3[k - 1].astype(F32)

    scores = full * inv_q * inv_d * (1.0 / TAU)
    expo = jnp.exp(scores)
    marks = hot[t]
    pos_hot, neg_hot = marks == 1.0, marks == 2.0
    stats[z] = rows8(
        pad_lanes(to_row(jnp.sum(expo, axis=1, keepdims=True)), 128),
        pad_lanes(to_row(jnp.sum(jnp.where(pos_hot, scores, 0.0), axis=1, keepdims=True)), 128),
        pad_lanes(to_row(jnp.sum(jnp.where(neg_hot, scores, 0.0), axis=1, keepdims=True)), 128),
    )
    def gather_start(ref, rid, pass_rid, each=1):
        for k in X_ORDER:
            push(ref(t), ref(t), rid + each * (4 - k), at_x(k))
        push(ref(t), ref(t), pass_rid, sib)

    def gather_pass(ref, pass_rid, k):
        slot = ref(2 * ((x + k) % NX) + c)
        push(slot, slot, pass_rid, sib)

    for k in Z_ORDER:
        push(stats.at[z], stats.at[z], R_STAT, at_z(k))
    cf[t] = (expo * inv_d).astype(BF16)
    gather_start(lambda i: cf.at[i], R_CF, R_CS)
    turn(6, 8)
    got(stats.at[pl.ds(0, NZ - 1)], R_STAT, sib)
    stat = stats[0]
    for k in range(1, NZ):
        stat = stat + stats[k]
    tot_row, pos_row, neg_row = stat[0:1, 0:nq], stat[1:2, 0:nq], stat[2:3, 0:nq]
    margin = neg_row - pos_row
    low = jnp.exp(-jnp.abs(margin))
    sig = jnp.where(margin >= 0.0, 1.0, low) / (1.0 + low)
    scale = (LOSS_SCALE / TAU) * inv_q_row
    row[t] = rows8(
        pad_lanes(scale / tot_row, 128),
        pad_lanes(scale * (jnp.exp(pos_row) / tot_row - (1.0 + sig)), 128),
        pad_lanes(scale * (jnp.exp(neg_row) / tot_row + sig), 128),
    )
    for k in range(1, NT):
        push(row.at[t], row.at[t], R_ROW, at_t(k))
    soft = jnp.maximum(margin, 0.0) + jnp.log1p(low)
    loss_part = jnp.sum(jnp.log(tot_row) - pos_row + soft, axis=1, keepdims=True)

    def make_coef(i):
        factors = row[i]
        coef = cf[i].astype(F32) * to_col(factors[0:1, 0:nq])
        marks = hot[i]
        coef = jnp.where(marks == 1.0, to_col(factors[1:2, 0:nq]) * inv_d, coef)
        coef = jnp.where(marks == 2.0, to_col(factors[2:3, 0:nq]) * inv_d, coef)
        return coef.astype(BF16)

    inner = make_coef(t).astype(F32) * full
    kz[z] = rows8(pad_lanes(to_row(jnp.sum(inner, axis=1, keepdims=True)), 128))
    kd[t] = rows8(jnp.sum(inner, axis=0, keepdims=True), jnp.broadcast_to(loss_part, (1, all_d)))
    to_owner = pltpu.make_async_remote_copy(
        src_ref=kz.at[z], dst_ref=kz.at[z], send_sem=send.at[1], recv_sem=recv.at[R_KZ],
        device_id=(y * NZ + t, t), device_id_type=MESH,
    )

    @pl.when(z != t)
    def _():
        to_owner.start()

    for k in range(1, NT):
        push(kd.at[t], kd.at[t], R_KD, at_t(k))
    for k in X_ORDER:
        got(cf.at[2 * ((x + k) % NX) + c], R_CF + k, at_x(k))
        gather_pass(lambda i: cf.at[i], R_CS, k)
    got(row.at[pl.ds(0, NT - 1)], R_ROW, sib)
    got(kd.at[pl.ds(0, NT - 1)], R_KD, sib)
    summed = kd[0]
    for k in range(1, NT):
        summed = summed + kd[k]
    summed = rows8(summed[0:1], summed[1:2], inv_d * inv_d)
    for k in range(NY):
        kds[k] = summed[:, k * nd : (k + 1) * nd]
    for k in Y_ORDER:
        push(kds.at[(y + k) % NY], ky.at[y], R_KY, at_y(k))
    ky[y] = kds[y]
    got(cf.at[pl.ds(0, NX)], R_CS, sib)
    for i in range(NT):
        cg[i] = make_coef(i)

    def grad_q(*offsets):
        rows = [cg[(z + k) % NZ] for k in offsets]
        grad = dot_nn(jnp.concatenate(rows, 0), dall[...].reshape(all_d, width))
        return [grad[i * nq : (i + 1) * nq] for i in range(len(offsets))]

    def second_stage():
        for i, k in enumerate((2, 6)):
            got(rq1.at[i], R_G1 + i, at_z(7 if k == 2 else 1))
            got(rqh.at[i], R_GH + i, at_z(8 - k))
            low = slice(0, half) if k == 2 else slice(half, nq)
            high = slice(half, nq) if k == 2 else slice(0, half)
            summed = hold[i] + rq1[i].astype(F32)
            sq[5 + i, low] = (summed[low] + rqh[i].astype(F32)).astype(BF16)
            sq[5 + i, high] = summed[high].astype(BF16)
            push(sq.at[5 + i], rq.at[3 - i], R_GQ, at_z(k))

    all_q = NZ * nq
    ct[...] = cg[...].reshape(all_q, all_d).T.reshape(NY, nd, all_q)
    rows = jnp.concatenate([ct[(y + k) % NY] for k in Y_ORDER + (0,)], 0)
    grad = dot_nn(rows, qall[...].reshape(all_q, width))
    d_halves = [pl.ds(i * (nd // 2), nd // 2) for i in range(2)]
    for i, k in enumerate(Y_ORDER):
        sd[k - 1] = grad[i * nd : (i + 1) * nd].astype(BF16)
    acc[nq:] = grad[3 * nd :]
    for half_at, rid in zip(d_halves, R_GD):
        for k in Y_ORDER:
            push(sd.at[k - 1, half_at], rd.at[3 - k, half_at], rid, at_y(k))
    for i, grad in enumerate(grad_q(3, 5, 4)):
        sq[i] = grad.astype(BF16)
    for i, k in enumerate((3, 5)):
        push(sq.at[i], rq1.at[i], R_G1 + i, at_z(1 if k == 3 else 7))
    push(sq.at[2, halves[2]], rqh.at[0], R_GH, at_z(2))
    push(sq.at[2, halves[6]], rqh.at[1], R_GH + 1, at_z(6))
    factor_copies = [
        pltpu.make_async_remote_copy(
            src_ref=kt, dst_ref=kt, send_sem=send.at[2], recv_sem=recv.at[R_KT],
            device_id=at_t(k), device_id_type=MESH,
        )
        for k in range(1, NT)
    ]

    @pl.when(z == t)
    def _():
        got(kz.at[pl.ds(0, NZ - 1)], R_KZ, sib)
        summed = kz[0]
        for k in range(1, NZ):
            summed = summed + kz[k]
        kt[...] = rows8(pad_lanes(summed[0:1, 0:nq] * inv_q_row * inv_q_row, 128))
        for copy in factor_copies:
            copy.start()

    first, second, third, fourth, own = grad_q(1, 7, 2, 6, 0)
    sq[3], sq[4] = first.astype(BF16), second.astype(BF16)
    for i, k in enumerate((1, 7)):
        push(sq.at[3 + i], rq.at[1 - i], R_GQ, at_z(k))
    hold[0], hold[1] = third, fourth
    acc[0:nq] = own
    got(ky.at[pl.ds(0, NY - 1)], R_KY, sib)
    summed = ky[0] + ky[1] + ky[2] + ky[3]
    loss_out[0, 0] = jnp.sum(summed[1:2, 0:1]) * (1.0 / (NY * NZ * nq))
    inverse2 = kds[y]
    factor = to_col(summed[0:1] * inverse2[2:3])
    for i in range(2):
        if i:
            second_stage()
        low, high = i * (nd // 2), (i + 1) * (nd // 2)
        got(rd.at[:, d_halves[i]], R_GD[i], sib)
        grad = acc[nq + low : nq + high]
        for k in (1, 2, 3):
            grad = grad + rd[k - 1, low:high].astype(F32)
        pre = gain * (grad - dall[y, low:high].astype(F32) * factor[low:high])
        gp[t, nq + low : nq + high] = pre.astype(BF16)
        gather_start(lambda j, i=i: gp.at[j, d_parts[i]], R_PD[i], R_PDS, 0)

    got(rq, R_GQ, sib)
    @pl.when(z != t)
    def _():
        got(kt, R_KT, sib)

    grad = acc[0:nq]
    for i in range(4):
        grad = grad + rq[i].astype(F32)
    factor = to_col(kt[0:1, 0:nq])
    gp[t, 0:nq] = (gain * (grad - qall[z].astype(F32) * factor)).astype(BF16)
    gather_start(lambda j: gp.at[j, q_rows], R_PQ, R_PQS)

    for i in range(2):
        got(gp.at[pl.ds(0, 3), d_parts[i]], R_PD[i], sib)
        for k in X_ORDER:
            gather_pass(lambda j, i=i: gp.at[j, d_parts[i]], R_PDS, k)
    result = None
    for a in (0, 1):
        if a:
            got(gp.at[pl.ds(0, NX), d_rows], R_PDS, sib)
        for k in (0,) + X_ORDER:
            owner = 2 * ((x + k) % NX) + (c + a) % 2
            term = dot_nn(gp[owner, nq:], wt[4 * a + k])
            result = term if result is None else result + term
    out[nq:] = result.astype(BF16)
    result = None
    for a in (0, 1):
        if a:
            got(gp.at[pl.ds(0, NX), q_rows], R_PQS, sib)
        for k in (0,) + X_ORDER:
            owner = 2 * ((x + k) % NX) + (c + a) % 2
            if k and not a:
                got(gp.at[owner, q_rows], R_PQ + k, at_x(k))
                gather_pass(lambda j: gp.at[j, q_rows], R_PQS, k)
            term = dot_nn(gp[owner, 0:nq], wt[4 * a + k])
            result = term if result is None else result + term
    out[0:nq] = result.astype(BF16)
    @pl.when(z != t)
    def _():
        to_owner.wait_send()

    @pl.when(z == t)
    def _():
        for copy in factor_copies:
            copy.wait_send()

    left = sum(sends) + (NZ // 2) * nq * width * 2
    views = (
        (depth * width * 2, NT, lambda n: wv.at[pl.ds(0, n)]),
        (width * 32, depth // 16, lambda n: wv.at[0, pl.ds(0, 16 * n)]),
        (4096, 4, lambda n: wv.at[0, pl.ds(0, 16), pl.ds(0, 128 * n)]),
    )
    for size, most, view in views:
        while left >= size:
            n = min(left // size, most)
            part = view(n)
            pltpu.make_async_remote_copy(
                src_ref=part, dst_ref=part, send_sem=send.at[0], recv_sem=recv.at[0],
                device_id=sib, device_id_type=MESH,
            ).wait_send()
            left -= n * size
    assert left == 0


def shards(
    query_residual, query_hidden, doc_residual, doc_hidden, down_weight, norm_gain, pos_index, neg_index,
):
    nq, width = query_residual.shape
    nd = doc_residual.shape[0]
    depth = query_hidden.shape[1]
    n = nq + nd
    all_q, all_d = NZ * nq, NY * nd
    hbm = pl.BlockSpec(memory_space=pltpu.HBM)
    vmem = pl.BlockSpec(memory_space=pltpu.VMEM)
    grads, loss = pl.pallas_call(
        functools.partial(kernel, nq, nd),
        out_shape=(pltpu.VMEM((n, depth), BF16), jax.ShapeDtypeStruct((1, 1), F32)),
        in_specs=[hbm] * 8,
        out_specs=(vmem, pl.BlockSpec(memory_space=pltpu.SMEM)),
        scratch_shapes=[
            pltpu.VMEM((NT, 1, width), F32),
            pltpu.VMEM((NZ * NY * nq // 128, 1, 128), jnp.int32),
            pltpu.VMEM((NZ * NY * nq // 128, 1, 128), jnp.int32),
            pltpu.VMEM((n, depth), BF16),
            pltpu.VMEM((n, width), BF16),
            pltpu.VMEM((NT, depth, width), BF16),
            pltpu.VMEM((NT, width, depth), BF16),
            pltpu.VMEM((NX, n, width), BF16),
            pltpu.VMEM((NX, n, width), BF16),
            pltpu.VMEM((NX - 1, n, width), BF16),
            pltpu.VMEM((NX - 1, n, width), BF16),
            pltpu.VMEM((n, width), F32),
            pltpu.VMEM((NZ, nq, width), BF16),
            pltpu.VMEM((NZ, nq, width), BF16),
            pltpu.VMEM((NY, nd, width), BF16),
            pltpu.VMEM((NY, nd, width), BF16),
            pltpu.VMEM((NX - 1, nq, all_d), BF16),
            pltpu.VMEM((NX - 1, nq, all_d), BF16),
            pltpu.VMEM((NX, 8, all_d), F32),
            pltpu.VMEM((NX - 1, 8, all_d), F32),
            pltpu.VMEM((NZ, 8, 128), F32),
            pltpu.VMEM((NT, 8, 128), F32),
            pltpu.VMEM((NT, nq, all_d), F32),
            pltpu.VMEM((NT, nq, all_d), BF16),
            pltpu.VMEM((NT, nq, all_d), BF16),
            pltpu.VMEM((NY, nd, all_q), BF16),
            pltpu.VMEM((NZ - 1, nq, width), BF16),
            pltpu.VMEM((2, nq, width), F32),
            pltpu.VMEM((2, nq, width), BF16),
            pltpu.VMEM((2, nq // 2, width), BF16),
            pltpu.VMEM((4, nq, width), BF16),
            pltpu.VMEM((NY - 1, nd, width), BF16),
            pltpu.VMEM((NY - 1, nd, width), BF16),
            pltpu.VMEM((NZ, 8, 128), F32),
            pltpu.VMEM((8, 128), F32),
            pltpu.VMEM((NT, 8, all_d), F32),
            pltpu.VMEM((NY, 8, nd), F32),
            pltpu.VMEM((NY, 8, nd), F32),
            pltpu.VMEM((NT, n, width), BF16),
            pltpu.SemaphoreType.DMA((16,)),
            pltpu.SemaphoreType.DMA((3,)),
            pltpu.SemaphoreType.DMA((RID.n,)),
        ],
        compiler_params=pltpu.CompilerParams(
            collective_id=0, has_side_effects=True, vmem_limit_bytes=62 * 2**20
        ),
        name="step",
    )(
        query_residual, query_hidden, doc_residual, doc_hidden, down_weight,
        norm_gain.reshape(NT, 1, width), pos_index.reshape(-1, 1, 128), neg_index.reshape(-1, 1, 128),
    )
    return grads[:nq], grads[nq:], loss.reshape(())


def solution(mesh):
    placed = (
        P("dp", "tensor"),
        P("dp", "tensor"),
        P("dp", "tensor"),
        P("dp", "tensor"),
        P("tensor", None),
        P(),
        P(),
        P(),
    )
    return jax.shard_map(
        shards,
        mesh=mesh,
        in_specs=placed,
        out_specs=(P("dp", "tensor"), P("dp", "tensor"), P()),
        check_vma=False,
    )
```

```python
import functools
import math

import jax
import jax.numpy as jnp
from jax import lax
from jax.experimental import pallas as pl
from jax.experimental.pallas import tpu as pltpu
from jax.sharding import PartitionSpec as P

EPS = 1e-06
TAU = 0.05
LOSS_SCALE = 256.0
NX, NY, NZ = 4, 4, 8
NT = 2 * NX
MESH = pl.DeviceIdType.MESH
F32 = jnp.float32
BF16 = jnp.bfloat16


def dot_nn(a, b):
    return lax.dot_general(a, b, (((1,), (0,)), ((), ())), preferred_element_type=F32)


def dot_nt(a, b):
    return lax.dot_general(a, b, (((1,), (1,)), ((), ())), preferred_element_type=F32)


def eye(n, m, shift=0):
    rows = lax.broadcasted_iota(jnp.int32, (n, m), 0)
    cols = lax.broadcasted_iota(jnp.int32, (n, m), 1)
    return cols == rows + shift


def to_row(col):
    n = col.shape[0]
    return jnp.sum(jnp.where(eye(n, n), col, 0.0), axis=0, keepdims=True)


def to_col(row):
    n = row.shape[1]
    return jnp.sum(jnp.where(eye(n, n), row, 0.0), axis=1, keepdims=True)


def rows8(*rows):
    width = rows[0].shape[1]
    index = lax.broadcasted_iota(jnp.int32, (8, width), 0)
    out = jnp.zeros((8, width), F32)
    for i, row in enumerate(rows):
        out = jnp.where(index == i, row, out)
    return out


def pad_lanes(row, width):
    return jnp.concatenate([row, jnp.zeros((1, width - row.shape[1]), F32)], axis=1)


class Ids:
    def __init__(self):
        self.n = 0

    def take(self, n):
        base = self.n
        self.n += n
        return base


RID = Ids()
R_SIB = RID.take(4)
R_XQ, R_XD = RID.take(1), (RID.take(1), RID.take(1))
R_Z2, R_Z6, R_Z1, R_Z3, R_QS = (RID.take(1) for _ in range(5))
R_YD, R_DS = (RID.take(1), RID.take(1)), RID.take(1)
R_SX, R_SS = RID.take(1), RID.take(1)
R_STAT, R_ROW = RID.take(1), RID.take(1)
R_CF, R_CS = RID.take(4), RID.take(1)
R_G1, R_GH, R_GQ = RID.take(2), RID.take(2), RID.take(1)
R_GD = (RID.take(1), RID.take(1))
R_KZ, R_KT, R_KD, R_KY = (RID.take(1) for _ in range(4))
R_PD, R_PDS, R_PQ, R_PQS = (RID.take(1), RID.take(1)), RID.take(1), RID.take(4), RID.take(1)
X_ORDER = (2, 1, 3)
Z_ORDER = (4, 3, 5, 2, 6, 1, 7)
Y_ORDER = (2, 1, 3)


def kernel(
    nq, nd, q_res, q_hid, d_res, d_hid, w_hbm, gain_hbm, pos_hbm, neg_hbm,
    out, loss_out,
    gain_ref, pos_ref, neg_ref, hid, res, wv, wt, s1, r1, s2, r2, acc, qall, qs, dall, ds, s3, r3, s3t, r3t, stats,
    row, hot, cf, cg, ct, sq, hold, rq1, rqh, rq, sd, rd, kz, kt, kd, kds, ky, gp, local, send, recv,
):
    dp = lax.axis_index("dp")
    t = lax.axis_index("tensor")
    x, c = t // 2, t % 2
    y, z = dp // NZ, dp % NZ

    def at_x(k):
        return (dp, 2 * ((x + k) % NX) + c)

    def at_t(k):
        return (dp, (t + k) % NT)

    def at_y(k):
        return (((y + k) % NY) * NZ + z, t)

    def at_z(k):
        return (y * NZ + (z + k) % NZ, t)

    sib = (dp, 2 * x + 1 - c)
    sends = []

    def push(src, dst, rid, device):
        copy = pltpu.make_async_remote_copy(
            src_ref=src, dst_ref=dst, send_sem=send.at[0], recv_sem=recv.at[rid],
            device_id=device, device_id_type=MESH,
        )
        copy.start()
        sends.append(math.prod(src.shape) * jnp.dtype(src.dtype).itemsize)

    def got(dst, rid, device):
        pltpu.make_async_remote_copy(
            src_ref=dst, dst_ref=dst, send_sem=send.at[0], recv_sem=recv.at[rid],
            device_id=device, device_id_type=MESH,
        ).wait_recv()

    def turn(first, last):
        for i in range(first, last):
            wt[i] = wv[i].T

    loads = []

    def load(src, dst):
        copy = pltpu.make_async_copy(src, dst, local.at[len(loads)])
        copy.start()
        loads.append(copy)
        return copy

    h_loads = [load(q_hid, hid.at[pl.ds(0, nq)]), load(d_hid, hid.at[pl.ds(nq, nd)])]
    x_all = X_ORDER + (0,)
    w_loads = {}
    depth, width = hid.shape[1], res.shape[1]
    steps = ((1, 2), (1, 1), (0, 2), (1, 3), (0, 1), (1, 0), (0, 3), (0, 0))
    for a, k in steps:
        owner = 2 * ((x + k) % NX) + (c + a) % 2
        columns = pl.ds(pl.multiple_of(owner * width, width), width)
        w_loads[a, k] = load(w_hbm.at[:, columns], wv.at[4 * a + k])
    r_loads = [load(gain_hbm, gain_ref), load(pos_hbm, pos_ref), load(neg_hbm, neg_ref)]
    r_loads += [load(q_res, res.at[pl.ds(0, nq)]), load(d_res, res.at[pl.ds(nq, nd)])]

    barrier = pltpu.get_barrier_semaphore()
    peers = [at_t(k) for k in range(1, NT)] + [at_z(k) for k in range(1, NZ)]
    peers += [at_y(k) for k in range(1, NY)]
    for peer in peers:
        pl.semaphore_signal(barrier, inc=1, device_id=peer, device_id_type=MESH)

    for copy in h_loads:
        copy.wait()
    q_rows, d_rows = pl.ds(0, nq), pl.ds(nq, nd)
    d_parts = [pl.ds(nq + i * (nd // 2), nd // 2) for i in range(2)]
    for i, (a, k) in enumerate(steps):
        w_loads[a, k].wait()
        part = dot_nn(hid[...], wv[4 * a + k])
        if a:
            s1[k] = part.astype(BF16)
            if i == 0:
                pl.semaphore_wait(barrier, len(peers))
            push(s1.at[k], r1.at[k], R_SIB + k, sib)
            continue
        got(r1.at[k], R_SIB + k, sib)
        part = part + r1[k].astype(F32)
        if k:
            s2[k - 1] = part.astype(BF16)
            push(s2.at[k - 1, q_rows], r2.at[3 - k, q_rows], R_XQ, at_x(k))
        else:
            acc[...] = part
        if k == 3:
            for place, rid in zip(d_parts, R_XD):
                for k in X_ORDER:
                    push(s2.at[k - 1, place], r2.at[3 - k, place], rid, at_x(k))
    for copy in r_loads:
        copy.wait()
    gain = gain_ref[t]

    parity = (z + c + 1) % 2

    def pass_q(k):
        slot = (z + k) % NZ
        copy = pltpu.make_async_remote_copy(
            src_ref=qall.at[slot], dst_ref=qs.at[slot], send_sem=send.at[0],
            recv_sem=recv.at[R_QS], device_id=sib, device_id_type=MESH,
        )

        @pl.when(parity == k % 2)
        def _():
            copy.start()

    def full_rows(rows):
        total = acc[rows] + res[rows].astype(F32)
        for k in (1, 2, 3):
            total = total + r2[k - 1, rows].astype(F32)
        return (total * gain).astype(BF16)

    got(r2.at[:, q_rows], R_XQ, sib)
    qall[z] = full_rows(slice(0, nq))
    for k in (2, 6, 1, 7):
        push(qall.at[z], qall.at[z], {2: R_Z6, 6: R_Z2}.get(k, R_Z1), at_z(k))
    pass_q(0)
    turn(0, 2)
    for i in range(2):
        got(r2.at[:, d_parts[i]], R_XD[i], sib)
        low = i * (nd // 2)
        dall[y, low : low + nd // 2] = full_rows(slice(nq + low, nq + low + nd // 2))
        slot = dall.at[y, pl.ds(low, nd // 2)]
        for k in Y_ORDER:
            push(slot, slot, R_YD[i], at_y(k))
        push(slot, ds.at[y, pl.ds(low, nd // 2)], R_DS, sib)
    half = nq // 2
    halves = {2: pl.ds(0, half), 6: pl.ds(half, half)}
    for k in (2, 6):
        slot = (z + k) % NZ
        got(qall.at[slot], R_Z2 if k == 2 else R_Z6, at_z(k))
        push(qall.at[slot], qall.at[slot], R_Z3, at_z(7 if k == 2 else 1))
        part = qall.at[slot, halves[k]]
        push(part, part, R_Z3, at_z(8 - k))
        pass_q(k)
    got(qall.at[pl.ds(0, 2)], R_Z1, sib)
    pass_q(1)
    pass_q(7)
    all_d = NY * nd
    lanes = lax.broadcasted_iota(jnp.int32, (1, all_d), 1)
    column = ((lanes // nd) * NZ + z) * nd + lanes % nd
    for i in range(NZ):
        at = y * (NZ * nq // 128) + i * nq // 128
        pick = eye(nq, 128, i * nq % 128)
        pos = jnp.sum(jnp.where(pick, pos_ref[at].astype(F32), 0.0), axis=1, keepdims=True)
        neg = jnp.sum(jnp.where(pick, neg_ref[at].astype(F32), 0.0), axis=1, keepdims=True)
        mark = jnp.where(column == neg.astype(jnp.int32), 2.0, 0.0)
        hot[i] = jnp.where(column == pos.astype(jnp.int32), 1.0, mark)
    turn(2, 4)

    for i in range(2):
        place = pl.ds(i * (nd // 2), nd // 2)
        got(dall.at[pl.ds(0, 3), place], R_YD[i], sib)
        for k in Y_ORDER:
            slot = (y + k) % NY
            push(dall.at[slot, place], ds.at[slot, place], R_DS, sib)
    got(qall.at[pl.ds(0, 3)], R_Z3, sib)
    for k in (3, 5, 4):
        pass_q(k)

    got(ds, R_DS, sib)

    def squares(*blocks):
        total = 0.0
        for rows in blocks:
            wide = rows.astype(F32)
            total = total + wide * wide
        return to_row(jnp.sum(total, axis=1, keepdims=True))

    got(qs.at[pl.ds(0, NZ // 2)], R_QS, sib)
    owners = [2 * ((x + k) % NX) + c for k in x_all]
    scores = dot_nt(jnp.concatenate([qall[i] for i in owners], 0), dall[...].reshape(all_d, width))
    scores = scores + dot_nt(jnp.concatenate([qs[i] for i in owners], 0), ds[...].reshape(all_d, width))
    for i, k in enumerate(X_ORDER):
        s3[k - 1] = scores[i * nq : (i + 1) * nq].astype(BF16)
        push(s3.at[k - 1], r3.at[3 - k], R_SX, at_x(k))
    own_scores = scores[3 * nq :]
    ss_d = jnp.concatenate([squares(dall[k], ds[k]) for k in range(NY)], axis=1)
    for k, owner in zip(x_all, owners):
        s3t[k] = rows8(pad_lanes(squares(qall[owner], qs[owner]), all_d), ss_d)
        if k:
            push(s3t.at[k], r3t.at[3 - k], R_SS, at_x(k))
    turn(4, 6)
    got(r3t, R_SS, sib)
    tail = s3t[0] + r3t[0] + r3t[1] + r3t[2]
    inv_d = lax.rsqrt(tail[1:2] + EPS)
    inv_q_row = lax.rsqrt(tail[0:1, 0:nq] + EPS)
    inv_q = to_col(inv_q_row)
    got(r3, R_SX, sib)
    full = own_scores
    for k in (1, 2, 3):
        full = full + r3[k - 1].astype(F32)

    scores = full * inv_q * inv_d * (1.0 / TAU)
    expo = jnp.exp(scores)
    marks = hot[t]
    pos_hot, neg_hot = marks == 1.0, marks == 2.0
    stats[z] = rows8(
        pad_lanes(to_row(jnp.sum(expo, axis=1, keepdims=True)), 128),
        pad_lanes(to_row(jnp.sum(jnp.where(pos_hot, scores, 0.0), axis=1, keepdims=True)), 128),
        pad_lanes(to_row(jnp.sum(jnp.where(neg_hot, scores, 0.0), axis=1, keepdims=True)), 128),
    )
    def gather_start(ref, rid, pass_rid, each=1):
        for k in X_ORDER:
            push(ref(t), ref(t), rid + each * (4 - k), at_x(k))
        push(ref(t), ref(t), pass_rid, sib)

    def gather_pass(ref, pass_rid, k):
        slot = ref(2 * ((x + k) % NX) + c)
        push(slot, slot, pass_rid, sib)

    for k in Z_ORDER:
        push(stats.at[z], stats.at[z], R_STAT, at_z(k))
    cf[t] = (expo * inv_d).astype(BF16)
    gather_start(lambda i: cf.at[i], R_CF, R_CS)
    turn(6, 8)
    got(stats.at[pl.ds(0, NZ - 1)], R_STAT, sib)
    stat = stats[0]
    for k in range(1, NZ):
        stat = stat + stats[k]
    tot_row, pos_row, neg_row = stat[0:1, 0:nq], stat[1:2, 0:nq], stat[2:3, 0:nq]
    margin = neg_row - pos_row
    low = jnp.exp(-jnp.abs(margin))
    sig = jnp.where(margin >= 0.0, 1.0, low) / (1.0 + low)
    scale = (LOSS_SCALE / TAU) * inv_q_row
    row[t] = rows8(
        pad_lanes(scale / tot_row, 128),
        pad_lanes(scale * (jnp.exp(pos_row) / tot_row - (1.0 + sig)), 128),
        pad_lanes(scale * (jnp.exp(neg_row) / tot_row + sig), 128),
    )
    for k in range(1, NT):
        push(row.at[t], row.at[t], R_ROW, at_t(k))
    soft = jnp.maximum(margin, 0.0) + jnp.log1p(low)
    loss_part = jnp.sum(jnp.log(tot_row) - pos_row + soft, axis=1, keepdims=True)

    def make_coef(i):
        factors = row[i]
        coef = cf[i].astype(F32) * to_col(factors[0:1, 0:nq])
        marks = hot[i]
        coef = jnp.where(marks == 1.0, to_col(factors[1:2, 0:nq]) * inv_d, coef)
        coef = jnp.where(marks == 2.0, to_col(factors[2:3, 0:nq]) * inv_d, coef)
        return coef.astype(BF16)

    inner = make_coef(t).astype(F32) * full
    kz[z] = rows8(pad_lanes(to_row(jnp.sum(inner, axis=1, keepdims=True)), 128))
    kd[t] = rows8(jnp.sum(inner, axis=0, keepdims=True), jnp.broadcast_to(loss_part, (1, all_d)))
    to_owner = pltpu.make_async_remote_copy(
        src_ref=kz.at[z], dst_ref=kz.at[z], send_sem=send.at[1], recv_sem=recv.at[R_KZ],
        device_id=(y * NZ + t, t), device_id_type=MESH,
    )

    @pl.when(z != t)
    def _():
        to_owner.start()

    for k in range(1, NT):
        push(kd.at[t], kd.at[t], R_KD, at_t(k))
    for k in X_ORDER:
        got(cf.at[2 * ((x + k) % NX) + c], R_CF + k, at_x(k))
        gather_pass(lambda i: cf.at[i], R_CS, k)
    got(row.at[pl.ds(0, NT - 1)], R_ROW, sib)
    got(kd.at[pl.ds(0, NT - 1)], R_KD, sib)
    summed = kd[0]
    for k in range(1, NT):
        summed = summed + kd[k]
    summed = rows8(summed[0:1], summed[1:2], inv_d * inv_d)
    for k in range(NY):
        kds[k] = summed[:, k * nd : (k + 1) * nd]
    for k in Y_ORDER:
        push(kds.at[(y + k) % NY], ky.at[y], R_KY, at_y(k))
    ky[y] = kds[y]
    got(cf.at[pl.ds(0, NX)], R_CS, sib)
    for i in range(NT):
        cg[i] = make_coef(i)

    def grad_q(*offsets):
        rows = [cg[(z + k) % NZ] for k in offsets]
        grad = dot_nn(jnp.concatenate(rows, 0), dall[...].reshape(all_d, width))
        return [grad[i * nq : (i + 1) * nq] for i in range(len(offsets))]

    def second_stage():
        for i, k in enumerate((2, 6)):
            got(rq1.at[i], R_G1 + i, at_z(7 if k == 2 else 1))
            got(rqh.at[i], R_GH + i, at_z(8 - k))
            low = slice(0, half) if k == 2 else slice(half, nq)
            high = slice(half, nq) if k == 2 else slice(0, half)
            summed = hold[i] + rq1[i].astype(F32)
            sq[5 + i, low] = (summed[low] + rqh[i].astype(F32)).astype(BF16)
            sq[5 + i, high] = summed[high].astype(BF16)
            push(sq.at[5 + i], rq.at[3 - i], R_GQ, at_z(k))

    all_q = NZ * nq
    ct[...] = cg[...].reshape(all_q, all_d).T.reshape(NY, nd, all_q)
    rows = jnp.concatenate([ct[(y + k) % NY] for k in Y_ORDER + (0,)], 0)
    grad = dot_nn(rows, qall[...].reshape(all_q, width))
    d_halves = [pl.ds(i * (nd // 2), nd // 2) for i in range(2)]
    for i, k in enumerate(Y_ORDER):
        sd[k - 1] = grad[i * nd : (i + 1) * nd].astype(BF16)
    acc[nq:] = grad[3 * nd :]
    for half_at, rid in zip(d_halves, R_GD):
        for k in Y_ORDER:
            push(sd.at[k - 1, half_at], rd.at[3 - k, half_at], rid, at_y(k))
    for i, grad in enumerate(grad_q(3, 5, 4)):
        sq[i] = grad.astype(BF16)
    for i, k in enumerate((3, 5)):
        push(sq.at[i], rq1.at[i], R_G1 + i, at_z(1 if k == 3 else 7))
    push(sq.at[2, halves[2]], rqh.at[0], R_GH, at_z(2))
    push(sq.at[2, halves[6]], rqh.at[1], R_GH + 1, at_z(6))
    factor_copies = [
        pltpu.make_async_remote_copy(
            src_ref=kt, dst_ref=kt, send_sem=send.at[2], recv_sem=recv.at[R_KT],
            device_id=at_t(k), device_id_type=MESH,
        )
        for k in range(1, NT)
    ]

    @pl.when(z == t)
    def _():
        got(kz.at[pl.ds(0, NZ - 1)], R_KZ, sib)
        summed = kz[0]
        for k in range(1, NZ):
            summed = summed + kz[k]
        kt[...] = rows8(pad_lanes(summed[0:1, 0:nq] * inv_q_row * inv_q_row, 128))
        for copy in factor_copies:
            copy.start()

    first, second, third, fourth, own = grad_q(1, 7, 2, 6, 0)
    sq[3], sq[4] = first.astype(BF16), second.astype(BF16)
    for i, k in enumerate((1, 7)):
        push(sq.at[3 + i], rq.at[1 - i], R_GQ, at_z(k))
    hold[0], hold[1] = third, fourth
    acc[0:nq] = own
    got(ky.at[pl.ds(0, NY - 1)], R_KY, sib)
    summed = ky[0] + ky[1] + ky[2] + ky[3]
    loss_out[0, 0] = jnp.sum(summed[1:2, 0:1]) * (1.0 / (NY * NZ * nq))
    inverse2 = kds[y]
    factor = to_col(summed[0:1] * inverse2[2:3])
    for i in range(2):
        if i:
            second_stage()
        low, high = i * (nd // 2), (i + 1) * (nd // 2)
        got(rd.at[:, d_halves[i]], R_GD[i], sib)
        grad = acc[nq + low : nq + high]
        for k in (1, 2, 3):
            grad = grad + rd[k - 1, low:high].astype(F32)
        pre = gain * (grad - dall[y, low:high].astype(F32) * factor[low:high])
        gp[t, nq + low : nq + high] = pre.astype(BF16)
        gather_start(lambda j, i=i: gp.at[j, d_parts[i]], R_PD[i], R_PDS, 0)

    got(rq, R_GQ, sib)
    @pl.when(z != t)
    def _():
        got(kt, R_KT, sib)

    grad = acc[0:nq]
    for i in range(4):
        grad = grad + rq[i].astype(F32)
    factor = to_col(kt[0:1, 0:nq])
    gp[t, 0:nq] = (gain * (grad - qall[z].astype(F32) * factor)).astype(BF16)
    gather_start(lambda j: gp.at[j, q_rows], R_PQ, R_PQS)

    for i in range(2):
        got(gp.at[pl.ds(0, 3), d_parts[i]], R_PD[i], sib)
        for k in X_ORDER:
            gather_pass(lambda j, i=i: gp.at[j, d_parts[i]], R_PDS, k)
    result = None
    for a in (0, 1):
        if a:
            got(gp.at[pl.ds(0, NX), d_rows], R_PDS, sib)
        for k in (0,) + X_ORDER:
            owner = 2 * ((x + k) % NX) + (c + a) % 2
            term = dot_nn(gp[owner, nq:], wt[4 * a + k])
            result = term if result is None else result + term
    out[nq:] = result.astype(BF16)
    result = None
    for a in (0, 1):
        if a:
            got(gp.at[pl.ds(0, NX), q_rows], R_PQS, sib)
        for k in (0,) + X_ORDER:
            owner = 2 * ((x + k) % NX) + (c + a) % 2
            if k and not a:
                got(gp.at[owner, q_rows], R_PQ + k, at_x(k))
                gather_pass(lambda j: gp.at[j, q_rows], R_PQS, k)
            term = dot_nn(gp[owner, 0:nq], wt[4 * a + k])
            result = term if result is None else result + term
    out[0:nq] = result.astype(BF16)
    @pl.when(z != t)
    def _():
        to_owner.wait_send()

    @pl.when(z == t)
    def _():
        for copy in factor_copies:
            copy.wait_send()

    left = sum(sends) + (NZ // 2) * nq * width * 2
    views = (
        (depth * width * 2, NT, lambda n: wv.at[pl.ds(0, n)]),
        (width * 32, depth // 16, lambda n: wv.at[0, pl.ds(0, 16 * n)]),
        (4096, 4, lambda n: wv.at[0, pl.ds(0, 16), pl.ds(0, 128 * n)]),
    )
    for size, most, view in views:
        while left >= size:
            n = min(left // size, most)
            part = view(n)
            pltpu.make_async_remote_copy(
                src_ref=part, dst_ref=part, send_sem=send.at[0], recv_sem=recv.at[0],
                device_id=sib, device_id_type=MESH,
            ).wait_send()
            left -= n * size
    assert left == 0


def split(nq, nd, grads, q_out, d_out, sem):
    d_copy = pltpu.make_async_copy(grads.at[pl.ds(nq, nd)], d_out, sem.at[0])
    q_copy = pltpu.make_async_copy(grads.at[pl.ds(0, nq)], q_out, sem.at[1])
    d_copy.start()
    q_copy.start()
    d_copy.wait()
    q_copy.wait()


def shards(
    query_residual, query_hidden, doc_residual, doc_hidden, down_weight, norm_gain, pos_index, neg_index,
):
    nq, width = query_residual.shape
    nd = doc_residual.shape[0]
    depth = query_hidden.shape[1]
    n = nq + nd
    all_q, all_d = NZ * nq, NY * nd
    hbm = pl.BlockSpec(memory_space=pltpu.HBM)
    vmem = pl.BlockSpec(memory_space=pltpu.VMEM)
    grads, loss = pl.pallas_call(
        functools.partial(kernel, nq, nd),
        out_shape=(pltpu.VMEM((n, depth), BF16), jax.ShapeDtypeStruct((1, 1), F32)),
        in_specs=[hbm] * 8,
        out_specs=(vmem, pl.BlockSpec(memory_space=pltpu.SMEM)),
        scratch_shapes=[
            pltpu.VMEM((NT, 1, width), F32),
            pltpu.VMEM((NZ * NY * nq // 128, 1, 128), jnp.int32),
            pltpu.VMEM((NZ * NY * nq // 128, 1, 128), jnp.int32),
            pltpu.VMEM((n, depth), BF16),
            pltpu.VMEM((n, width), BF16),
            pltpu.VMEM((NT, depth, width), BF16),
            pltpu.VMEM((NT, width, depth), BF16),
            pltpu.VMEM((NX, n, width), BF16),
            pltpu.VMEM((NX, n, width), BF16),
            pltpu.VMEM((NX - 1, n, width), BF16),
            pltpu.VMEM((NX - 1, n, width), BF16),
            pltpu.VMEM((n, width), F32),
            pltpu.VMEM((NZ, nq, width), BF16),
            pltpu.VMEM((NZ, nq, width), BF16),
            pltpu.VMEM((NY, nd, width), BF16),
            pltpu.VMEM((NY, nd, width), BF16),
            pltpu.VMEM((NX - 1, nq, all_d), BF16),
            pltpu.VMEM((NX - 1, nq, all_d), BF16),
            pltpu.VMEM((NX, 8, all_d), F32),
            pltpu.VMEM((NX - 1, 8, all_d), F32),
            pltpu.VMEM((NZ, 8, 128), F32),
            pltpu.VMEM((NT, 8, 128), F32),
            pltpu.VMEM((NT, nq, all_d), F32),
            pltpu.VMEM((NT, nq, all_d), BF16),
            pltpu.VMEM((NT, nq, all_d), BF16),
            pltpu.VMEM((NY, nd, all_q), BF16),
            pltpu.VMEM((NZ - 1, nq, width), BF16),
            pltpu.VMEM((2, nq, width), F32),
            pltpu.VMEM((2, nq, width), BF16),
            pltpu.VMEM((2, nq // 2, width), BF16),
            pltpu.VMEM((4, nq, width), BF16),
            pltpu.VMEM((NY - 1, nd, width), BF16),
            pltpu.VMEM((NY - 1, nd, width), BF16),
            pltpu.VMEM((NZ, 8, 128), F32),
            pltpu.VMEM((8, 128), F32),
            pltpu.VMEM((NT, 8, all_d), F32),
            pltpu.VMEM((NY, 8, nd), F32),
            pltpu.VMEM((NY, 8, nd), F32),
            pltpu.VMEM((NT, n, width), BF16),
            pltpu.SemaphoreType.DMA((16,)),
            pltpu.SemaphoreType.DMA((3,)),
            pltpu.SemaphoreType.DMA((RID.n,)),
        ],
        compiler_params=pltpu.CompilerParams(
            collective_id=0, has_side_effects=True, vmem_limit_bytes=62 * 2**20
        ),
        name="step",
    )(
        query_residual, query_hidden, doc_residual, doc_hidden, down_weight,
        norm_gain.reshape(NT, 1, width), pos_index.reshape(-1, 1, 128), neg_index.reshape(-1, 1, 128),
    )
    query_grad, doc_grad = pl.pallas_call(
        functools.partial(split, nq, nd),
        out_shape=(jax.ShapeDtypeStruct((nq, depth), BF16), jax.ShapeDtypeStruct((nd, depth), BF16)),
        in_specs=[vmem],
        out_specs=(hbm, hbm),
        scratch_shapes=[pltpu.SemaphoreType.DMA((2,))],
        name="split",
    )(grads)
    return query_grad, doc_grad, loss.reshape(())


def solution(mesh):
    placed = (
        P("dp", "tensor"),
        P("dp", "tensor"),
        P("dp", "tensor"),
        P("dp", "tensor"),
        P("tensor", None),
        P(),
        P(),
        P(),
    )
    return jax.shard_map(
        shards,
        mesh=mesh,
        in_specs=placed,
        out_specs=(P("dp", "tensor"), P("dp", "tensor"), P()),
        check_vma=False,
    )
```
